512 devices in a mesh: group: 4 (over z_lo), seq: 16 (over y, core), tp: 8 (over z_hi, x).
Axes of the slice: x: 4, y: 8, z: 8 (z_hi: 2, z_lo: 4; z = z_hi * 4 + z_lo), core: 2. Of those that a mesh axis runs over, the one named last changes fastest.
Arguments:
- queries: bfloat16 [8192, 8, 8, 128], P('seq', 'tp', 'group'), may hold values from -384 to 384
- aug_states: bfloat16 [8192, 5120], P('seq', ('group', 'tp')), may hold values from -6 to 6
- key_value_weight: bfloat16 [5120, 8, 2, 128], P(('group', 'tp')), may hold values from -0.078125 to 0.078125
- block_order: int32 [32], replicated, may hold values from 0 to 31, each once
Outputs:
- context: bfloat16 [8192, 8, 8, 128], P('seq', 'tp', 'group')
The draws below stay inside these ranges and needn't reach their ends.
Inputs may be any that keep to these rules, and one draw needn't show every extreme that they name: `block_order`: each storage block number appears once.
All inputs are finite; a program needn't handle non-finite values.
Results may differ from the reference program's by a relative error of at most 0.01.
The reference program's roundings to bfloat16 on the way (of `kv` and `probs`) count: a program that leaves them out, or rounds other values in their place, can miss the bound.
Values may be sent and summed in bfloat16 or wider, within the bound.
A program may use at most 128 MiB of HBM per device.

```python
import jax
import jax.numpy as jnp
from jax import lax

DA = 5120
KVH = 8
QPK = 8
HD = 128
TOK_DEV = 512
TOKENS = 8192
N_SEQ = 16


def draw_queries(key, part):
    key = jax.random.fold_in(key, 11)
    base_key = jax.random.fold_in(key, 0)
    values = jnp.clip(jax.random.normal(base_key, (TOKENS, KVH, QPK, HD), jnp.float32), -6.0, 6.0)
    return values.astype(jnp.bfloat16)


def block_scale(own_key, dims, shards, least, largest):
    level = 1.0
    for position, blocks in shards:
        heights = jax.random.uniform(jax.random.fold_in(jax.random.fold_in(own_key, 6), position), (blocks,), jnp.float32, least / len(shards), largest / len(shards))
        level = level * jnp.repeat(jnp.exp(heights), dims[position] // blocks).reshape((-1,) + (1,) * (len(dims) - 1 - position))
    return level


def normal_values(stream_key, dims, width, limit, cuts=(), kind=jnp.bfloat16):
    level = block_scale(stream_key, dims, cuts, -0.22, 0.18) if cuts else 1.0
    drawn = jax.random.normal(stream_key, dims, jnp.float32) * width * level
    return jnp.minimum(jnp.maximum(drawn, -limit), limit).astype(kind)


def setup_inputs(seed: int = 0) -> dict:
    streams_of = jax.random.split(jax.random.key(seed), 5)
    queries = draw_queries(jax.random.fold_in(streams_of[4], 71), 0)
    aug_states = normal_values(streams_of[1], (TOKENS, DA), 1.0, 6.0, ((0, 16), (1, 32)))
    key_value_weight = normal_values(streams_of[2], (DA, KVH, 2, HD), DA ** -0.5, 0.078125, ((0, 32),))
    block_order = jax.random.permutation(streams_of[3], 2 * N_SEQ).astype(jnp.int32)
    return {"queries": queries, "aug_states": aug_states, "key_value_weight": key_value_weight, "block_order": block_order}


def positions(block_order, count, half):
    rows = jnp.arange(count, dtype=jnp.int32)
    return block_order[rows // half] * half + rows % half


def reference(queries, aug_states, key_value_weight, block_order):
    flat_weight = key_value_weight.reshape(DA, KVH * 2 * HD)
    kv = jnp.dot(aug_states, flat_weight, preferred_element_type=jnp.float32).astype(jnp.bfloat16)
    kv = kv.reshape(TOKENS, KVH, 2, HD)
    pos = positions(block_order, TOKENS, TOK_DEV // 2)
    scale = HD ** -0.5
    keys_all = jnp.transpose(kv[:, :, 0, :], (1, 0, 2))
    values_all = jnp.transpose(kv[:, :, 1, :], (1, 0, 2))
    query_heads = jnp.transpose(queries, (1, 0, 2, 3)).reshape(KVH, N_SEQ, TOK_DEV, QPK, HD)
    pos_blocks = pos.reshape(N_SEQ, TOK_DEV)

    def one_head(items):
        query_head, keys, values = items
        keys32 = keys.astype(jnp.float32)
        values32 = values.astype(jnp.float32)

        def one_block(inner):
            query_block, block_pos = inner
            scores = jnp.einsum("rqe,ue->qru", query_block.astype(jnp.float32), keys32) * scale
            kept = pos[None, None, :] <= block_pos[None, :, None]
            scores = jnp.where(kept, scores, -1e30)
            top = jnp.max(scores, axis=-1, keepdims=True)
            weights = jnp.where(kept, jnp.exp(scores - top), 0.0)
            total = jnp.sum(weights, axis=-1)
            probs = weights.astype(jnp.bfloat16)
            summed = jnp.einsum("qru,ue->qre", probs.astype(jnp.float32), values32)
            out = (summed / total[..., None]).astype(jnp.bfloat16)
            return jnp.transpose(out, (1, 0, 2))

        return lax.map(one_block, (query_head, pos_blocks))

    result = lax.map(one_head, (query_heads, keys_all, values_all))
    result = jnp.transpose(result, (1, 2, 0, 3, 4))
    return result.reshape(TOKENS, KVH, QPK, HD)
```

```python
import functools

import jax
import jax.numpy as jnp
from jax import lax
from jax.experimental import pallas as pl
from jax.experimental.pallas import tpu as pltpu
from jax.sharding import PartitionSpec as P

MESH = pl.DeviceIdType.MESH
NX, NY, NZ, NG = 4, 8, 8, 4
QT = 128
ROWS = 256
NEG = -1e30
LOG2E = 1.4426950408889634


def kernel(
    order_ref,
    q_ref,
    aug_ref,
    w_ref,
    out_ref,
    augx,
    wx,
    op,
    om,
    ip,
    im,
    own,
    kvs,
    m_ref,
    l_ref,
    acc_ref,
    ax_s,
    ax_r,
    wx_s,
    wx_r,
    ws_s,
    ws_r,
    rp_s,
    rp_r,
    rm_s,
    rm_r,
    zg_s,
    zg_r,
    yp_s,
    yp_r,
    ym_s,
    ym_r,
    sb_s,
    sb_r,
    loc,
):
    g = lax.axis_index("group")
    seq = lax.axis_index("seq")
    tp = lax.axis_index("tp")
    y, c = lax.div(seq, 2), lax.rem(seq, 2)
    zh, x = lax.div(tp, NX), lax.rem(tp, NX)
    z = zh * NG + g

    def dev(z=z, y=y, c=c, x=x):
        return (lax.rem(z, NG), y * 2 + c, lax.div(z, NG) * NX + x)

    def remote(src, dst, send, recv, to):
        return pltpu.make_async_remote_copy(
            src_ref=src, dst_ref=dst, send_sem=send, recv_sem=recv, device_id=to, device_id_type=MESH
        )

    def wrap(v, n):
        return lax.rem(v + 4 * n, n)

    x_to = [dev(x=wrap(x + d, NX)) for d in (1, 2, 3)]
    z_next, z_prev = dev(z=wrap(z + 1, NZ)), dev(z=wrap(z - 1, NZ))
    g_to = [dev(z=zh * NG + wrap(g + d, NG)) for d in (1, 2, 3)]
    y_next, y_prev = dev(y=wrap(y + 1, NY)), dev(y=wrap(y - 1, NY))
    sib = dev(c=1 - c)

    barrier = pltpu.get_barrier_semaphore()
    partners = x_to + [z_next, z_prev] + g_to + [y_next, y_prev, sib]
    for to in partners:
        pl.semaphore_signal(barrier, inc=1, device_id=to, device_id_type=MESH)

    own_w = [
        pltpu.make_async_copy(w_ref.at[:, pl.ds(pl.multiple_of((x + NX * h) * 2 * QT, 2 * QT), 2 * QT)], wx.at[h, x], loc.at[h]) for h in (0, 1)
    ]
    own_a = [
        pltpu.make_async_copy(aug_ref.at[:, pl.ds(i * QT, QT)], augx.at[i, x], loc.at[2 + i])
        for i in range(NG)
    ]
    for cp in own_w + own_a:
        cp.start()
    pl.semaphore_wait(barrier, len(partners))

    w_sends = []
    for i, d in enumerate((1, 2, 3)):
        to_x = wrap(x + d, NX)
        cp = remote(w_ref.at[:, pl.ds(pl.multiple_of((to_x + NX * c) * 2 * QT, 2 * QT), 2 * QT)], wx.at[c, x], wx_s.at[i], wx_r.at[i], x_to[i])
        cp.start()
        w_sends.append(cp)
    quarters = [g, wrap(g - 1, NG), wrap(g + 1, NG), wrap(g + 2, NG)]
    a_sends = []
    for j, qt in enumerate(quarters):
        for i in range(3):
            cp = remote(
                aug_ref.at[:, pl.ds(pl.multiple_of(qt * QT, QT), QT)],
                augx.at[qt, x],
                ax_s.at[j, i],
                ax_r.at[j, i],
                x_to[i],
            )
            cp.start()
            a_sends.append(cp)
    w_shares = []
    for i, d in enumerate((1, 2, 3)):
        src = wrap(x - d, NX)
        remote(wx.at[c, src], wx.at[c, src], wx_s.at[i], wx_r.at[i], x_to[i]).wait_recv()
        cp = remote(wx.at[c, src], wx.at[c, src], ws_s.at[i], ws_r.at[i], sib)
        cp.start()
        w_shares.append(cp)
    for cp in own_w + own_a:
        cp.wait()
    for i, d in enumerate((1, 2, 3)):
        src = wrap(x - d, NX)
        remote(wx.at[1 - c, src], wx.at[1 - c, src], ws_s.at[i], ws_r.at[i], sib).wait_recv()

    def arrive_states(j):
        for i, d in enumerate((1, 2, 3)):
            slot = augx.at[quarters[j], wrap(x - d, NX)]
            remote(slot, slot, ax_s.at[j, i], ax_r.at[j, i], x_to[i]).wait_recv()

    def share(target):
        states = augx[lax.rem(target, NG)].reshape(NX * 160, QT)
        weights = wx[lax.div(target, NG)].reshape(NX * 160, 2 * QT)
        return lax.dot_general(
            states, weights, (((0,), (0,)), ((), ())), preferred_element_type=jnp.float32
        )

    sends = []

    def send_p(k, half):
        cp = remote(op.at[k - 1, half], ip.at[k - 1, half], rp_s.at[k - 1, half], rp_r.at[k - 1, half], z_next)
        cp.start()
        sends.append(cp)

    def send_m(k, half):
        cp = remote(om.at[k - 1, half], im.at[k - 1, half], rm_s.at[k - 1, half], rm_r.at[k - 1, half], z_prev)
        cp.start()
        sends.append(cp)

    def got_p(k, half):
        slot = ip.at[k - 1, half]
        remote(slot, slot, rp_s.at[k - 1, half], rp_r.at[k - 1, half], z_next).wait_recv()
        return ip[k - 1, half]

    def got_m(k, half):
        slot = im.at[k - 1, half]
        remote(slot, slot, rm_s.at[k - 1, half], rm_r.at[k - 1, half], z_prev).wait_recv()
        return im[k - 1, half]

    arrive_states(0)
    part = share(wrap(z + 4, NZ))
    op[3, 0] = part[:, :QT]
    om[3, 1] = part[:, QT:]
    send_p(4, 0)
    send_m(4, 1)
    arrive_states(1)
    part = share(wrap(z + 3, NZ))
    op[2, 1] = part[:, QT:]
    send_p(3, 1)
    op[2, 0] = part[:, :QT]
    arrive_states(2)
    part = share(wrap(z - 3, NZ))
    om[2, 0] = part[:, :QT]
    send_m(3, 0)
    om[2, 1] = part[:, QT:]
    arrive_states(3)
    part = share(wrap(z + 2, NZ))
    op[1, 0] = part[:, :QT]
    op[1, 1] = part[:, QT:]
    part = share(wrap(z - 2, NZ))
    om[1, 0] = part[:, :QT]
    om[1, 1] = part[:, QT:]
    op[2, 0] += got_p(4, 0)
    send_p(3, 0)
    om[2, 1] += got_m(4, 1)
    send_m(3, 1)
    part = share(wrap(z + 1, NZ))
    op[0, 0] = part[:, :QT]
    op[0, 1] = part[:, QT:]
    part = share(wrap(z - 1, NZ))
    om[0, 0] = part[:, :QT]
    om[0, 1] = part[:, QT:]
    own[...] = share(z)
    for k in (3, 2):
        for first in (0, 1):
            hp, hm = 1 - first, first
            op[k - 2, hp] += got_p(k, hp)
            send_p(k - 1, hp)
            om[k - 2, hm] += got_m(k, hm)
            send_m(k - 1, hm)

    low = own[:, :QT] + got_m(1, 0)
    high = own[:, QT:] + got_p(1, 1)
    low += got_p(1, 0)
    high += got_m(1, 1)
    kvs[y, c, g, :, :QT] = low.astype(jnp.bfloat16)
    kvs[y, c, g, :, QT:] = high.astype(jnp.bfloat16)

    for i in range(3):
        slot = kvs.at[y, c, g]
        cp = remote(slot, slot, zg_s.at[i], zg_r.at[i], g_to[i])
        cp.start()
        sends.append(cp)

    def ring_p(d, qi, qt):
        slot = kvs.at[wrap(y - d, NY), c, qt]
        return remote(slot, slot, yp_s.at[d, qi], yp_r.at[d, qi], y_next)

    def ring_m(d, qi, qt):
        slot = kvs.at[wrap(y + d, NY), c, qt]
        return remote(slot, slot, ym_s.at[d, qi], ym_r.at[d, qi], y_prev)

    for i in range(NG):
        qt = wrap(g - i, NG)
        if i > 0:
            slot = kvs.at[y, c, qt]
            remote(slot, slot, zg_s.at[i - 1], zg_r.at[i - 1], g_to[i - 1]).wait_recv()
        ring_p(0, qt, qt).start()
        ring_m(0, qt, qt).start()

    def sibling(yi, ci, idx):
        slot = kvs.at[yi, ci]
        return remote(slot, slot, sb_s.at[idx], sb_r.at[idx], sib)

    sibling(y, c, y).start()

    scale = LOG2E * 128 ** -0.5

    def attend(yi, ci, diagonal=False):
        def rows_of(rb, carry):
            base = pl.multiple_of(rb * ROWS, ROWS)
            a = lax.div(rb, 512 // ROWS)
            qo = order_ref[2 * seq + a]
            q = q_ref[pl.ds(base, ROWS), :]
            block = kvs.at[yi, ci].reshape(4 * QT, 2 * QT)
            keys = block[:, :QT]
            values = block[:, QT:]
            s = lax.dot_general(q, keys, (((1,), (1,)), ((), ())), preferred_element_type=jnp.float32)
            if diagonal:
                row = lax.broadcasted_iota(jnp.int32, (ROWS, 256), 0) + lax.rem(rb, 512 // ROWS) * ROWS
                row = lax.shift_right_logical(row, 1)
                col = lax.broadcasted_iota(jnp.int32, (ROWS, 256), 1)
                parts = []
                for h in (0, 1):
                    ko = order_ref[2 * (yi * 2 + ci) + h]
                    kept = ko * 256 + col <= qo * 256 + row
                    parts.append(jnp.where(kept, s[:, h * 256 : (h + 1) * 256], NEG))
                top = jnp.max(jnp.maximum(parts[0], parts[1]), axis=-1, keepdims=True)
                new = top
                shifted = [(p - new) * scale for p in parts]
            else:
                old = m_ref[pl.ds(base, ROWS), :]
                parts = [s[:, h * 256 : (h + 1) * 256] for h in (0, 1)]
                new = old[:, :1]
                bias = []
                for h in (0, 1):
                    ko = order_ref[2 * (yi * 2 + ci) + h]
                    b = jnp.where(ko < qo, 0.0, NEG)
                    bias.append(b)
                    new = jnp.maximum(new, jnp.max(parts[h], axis=-1, keepdims=True) + b)
                shifted = [(parts[h] - (new - bias[h])) * scale for h in (0, 1)]
            p = [jnp.exp2(v) for v in shifted]
            total = p[0][:, :128] + p[0][:, 128:] + p[1][:, :128] + p[1][:, 128:]
            probs = jnp.concatenate([v.astype(jnp.bfloat16) for v in p], axis=1)
            o = jnp.dot(probs, values, preferred_element_type=jnp.float32)
            if diagonal:
                l_ref[pl.ds(base, ROWS), :] = total
                acc_ref[pl.ds(base, ROWS), :] = o
            else:
                alpha = jnp.exp2((old[:, :1] - new) * scale)
                l_ref[pl.ds(base, ROWS), :] = l_ref[pl.ds(base, ROWS), :] * alpha + total
                acc_ref[pl.ds(base, ROWS), :] = acc_ref[pl.ds(base, ROWS), :] * alpha + o
            m_ref[pl.ds(base, ROWS), :] = jnp.broadcast_to(new, (ROWS, 128))
            return carry

        lax.fori_loop(0, 1024 // ROWS, rows_of, 0)

    attend(y, c, True)

    def wait_sibling(yi):
        sibling(yi, 1 - c, yi).wait_recv()

    def step(d, carry):
        last_p, last_m = wrap(y - d + 1, NY), wrap(y + d - 1, NY)
        new_p, new_m = wrap(y - d, NY), wrap(y + d, NY)
        for qt in range(NG):
            ring_p_slot = kvs.at[new_p, c, qt]
            ring_m_slot = kvs.at[new_m, c, qt]
            remote(ring_p_slot, ring_p_slot, yp_s.at[d - 1, qt], yp_r.at[d - 1, qt], y_next).wait_recv()

            @pl.when((d < 3) | (qt < 2))
            def _():
                ring_p(d, qt, qt).start()

            remote(ring_m_slot, ring_m_slot, ym_s.at[d - 1, qt], ym_r.at[d - 1, qt], y_prev).wait_recv()

            @pl.when((d < 3) | (qt >= 2))
            def _():
                ring_m(d, qt, qt).start()

            if qt == 0:

                @pl.when(d > 1)
                def _():
                    attend(last_p, c)

            elif qt == 1:

                @pl.when(d > 1)
                def _():
                    attend(last_m, c)

            elif qt == 2:
                wait_sibling(last_p)
                attend(last_p, 1 - c)
            else:

                @pl.when(d > 1)
                def _():
                    wait_sibling(last_m)
                    attend(last_m, 1 - c)

        sibling(new_p, c, new_p).start()
        sibling(new_m, c, new_m).start()
        return carry

    lax.fori_loop(1, 4, step, 0)
    far = wrap(y + 4, NY)
    for n, (qp, qm) in enumerate(((0, 2), (1, 3))):
        slot = kvs.at[far, c, qp]
        remote(slot, slot, yp_s.at[3, qp], yp_r.at[3, qp], y_next).wait_recv()
        slot = kvs.at[far, c, qm]
        remote(slot, slot, ym_s.at[3, qm], ym_r.at[3, qm], y_prev).wait_recv()
        if n == 0:
            attend(wrap(y - 3, NY), c)
            attend(wrap(y + 3, NY), c)
    sibling(far, c, far).start()
    wait_sibling(wrap(y - 3, NY))
    attend(wrap(y - 3, NY), 1 - c)
    wait_sibling(wrap(y + 3, NY))
    attend(wrap(y + 3, NY), 1 - c)
    attend(far, c)
    wait_sibling(far)
    attend(far, 1 - c)

    total = jnp.sum(l_ref[...], axis=-1, keepdims=True)
    out_ref[...] = (acc_ref[...] / total).astype(jnp.bfloat16)

    for cp in w_sends + a_sends + w_shares + sends:
        cp.wait_send()

    def drain(d, carry):
        for qt in range(NG):

            @pl.when((d < 3) | (qt < 2))
            def _():
                ring_p(d, qt, qt).wait_send()

            @pl.when((d < 3) | (qt >= 2))
            def _():
                ring_m(d, qt, qt).wait_send()

        return carry

    lax.fori_loop(0, 4, drain, 0)

    def drain_sibling(yi, carry):
        sibling(yi, c, yi).wait_send()
        return carry

    lax.fori_loop(0, NY, drain_sibling, 0)


def body(queries, aug_states, key_value_weight, block_order):
    tok = queries.shape[0]
    rows = tok * queries.shape[2]
    q = queries.reshape(rows, 128)
    aug = aug_states.T
    w = key_value_weight.reshape(160, 2048)
    dma = pltpu.SemaphoreType.DMA
    out = pl.pallas_call(
        kernel,
        out_shape=jax.ShapeDtypeStruct((rows, 128), jnp.bfloat16),
        in_specs=[pl.BlockSpec(memory_space=pltpu.SMEM)] + [pl.BlockSpec(memory_space=pltpu.VMEM)] * 3,
        out_specs=pl.BlockSpec(memory_space=pltpu.VMEM),
        scratch_shapes=[
            pltpu.VMEM((NG, NX, 160, QT), jnp.bfloat16),
            pltpu.VMEM((2, NX, 160, 2 * QT), jnp.bfloat16),
            pltpu.VMEM((4, 2, QT, QT), jnp.float32),
            pltpu.VMEM((4, 2, QT, QT), jnp.float32),
            pltpu.VMEM((4, 2, QT, QT), jnp.float32),
            pltpu.VMEM((4, 2, QT, QT), jnp.float32),
            pltpu.VMEM((QT, 2 * QT), jnp.float32),
            pltpu.VMEM((NY, 2, NG, QT, 2 * QT), jnp.bfloat16),
            pltpu.VMEM((rows, 128), jnp.float32),
            pltpu.VMEM((rows, 128), jnp.float32),
            pltpu.VMEM((rows, 128), jnp.float32),
            dma((4, 3)),
            dma((4, 3)),
            dma((3,)),
            dma((3,)),
            dma((3,)),
            dma((3,)),
            dma((4, 2)),
            dma((4, 2)),
            dma((4, 2)),
            dma((4, 2)),
            dma((3,)),
            dma((3,)),
            dma((4, 4)),
            dma((4, 4)),
            dma((4, 4)),
            dma((4, 4)),
            dma((8,)),
            dma((8,)),
            dma((6,)),
        ],
        compiler_params=pltpu.CompilerParams(
            collective_id=0, has_side_effects=True, vmem_limit_bytes=40 * 1024 * 1024
        ),
        cost_estimate=pl.CostEstimate(flops=9 * 10**9, bytes_accessed=2 * 10**6, transcendentals=8 * 10**6),
        name="compose",
    )(block_order, q, aug, w)
    return out.reshape(queries.shape)


def solution(mesh):
    in_specs = (
        P("seq", "tp", "group", None),
        P("seq", ("group", "tp")),
        P(("group", "tp"), None, None, None),
        P(),
    )
    out_specs = P("seq", "tp", "group", None)
    return jax.shard_map(body, mesh=mesh, in_specs=in_specs, out_specs=out_specs, check_vma=False)
```

```python
import functools

import jax
import jax.numpy as jnp
from jax import lax
from jax.experimental import pallas as pl
from jax.experimental.pallas import tpu as pltpu
from jax.sharding import PartitionSpec as P

MESH = pl.DeviceIdType.MESH
NX, NY, NZ, NG = 4, 8, 8, 4
QT = 128
ROWS = 256
NEG = -1e30
LOG2E = 1.4426950408889634


def kernel(
    order_ref,
    q_hbm,
    aug_hbm,
    w_hbm,
    out_ref,
    q_ref,
    aug_ref,
    w_ref,
    w_wide,
    w_heads,
    augx,
    wx,
    op,
    om,
    ip,
    im,
    own,
    kvs,
    m_ref,
    l_ref,
    acc_ref,
    sc0,
    sc1,
    ax_s,
    ax_r,
    wx_s,
    wx_r,
    ws_s,
    ws_r,
    rp_s,
    rp_r,
    rm_s,
    rm_r,
    zg_s,
    zg_r,
    zq_s,
    zq_r,
    yp_s,
    yp_r,
    ym_s,
    ym_r,
    sb_s,
    sb_r,
    loc,
):
    g = lax.axis_index("group")
    seq = lax.axis_index("seq")
    tp = lax.axis_index("tp")
    y, c = lax.div(seq, 2), lax.rem(seq, 2)
    zh, x = lax.div(tp, NX), lax.rem(tp, NX)
    z = zh * NG + g

    def dev(z=z, y=y, c=c, x=x):
        return (lax.rem(z, NG), y * 2 + c, lax.div(z, NG) * NX + x)

    def remote(src, dst, send, recv, to):
        return pltpu.make_async_remote_copy(
            src_ref=src, dst_ref=dst, send_sem=send, recv_sem=recv, device_id=to, device_id_type=MESH
        )

    def wrap(v, n):
        return lax.rem(v + 4 * n, n)

    x_to = [dev(x=wrap(x + d, NX)) for d in (1, 2, 3)]
    z_next, z_prev = dev(z=wrap(z + 1, NZ)), dev(z=wrap(z - 1, NZ))
    g1, g2, g3 = g + 1 - 2 * lax.rem(g, 2), lax.rem(g + 2, NG), 3 - g
    g_to = [dev(z=zh * NG + v) for v in (g1, g2, g3)]
    y_next, y_prev = dev(y=wrap(y + 1, NY)), dev(y=wrap(y - 1, NY))
    sib = dev(c=1 - c)

    barrier = pltpu.get_barrier_semaphore()
    partners = x_to + [z_next, z_prev] + g_to + [y_next, y_prev, sib]
    for to in partners:
        pl.semaphore_signal(barrier, inc=1, device_id=to, device_id_type=MESH)

    loads = [
        pltpu.make_async_copy(w_hbm, w_ref, loc.at[0]),
        pltpu.make_async_copy(aug_hbm, aug_ref, loc.at[1]),
        pltpu.make_async_copy(q_hbm, q_ref, loc.at[2]),
    ]
    for cp in loads:
        cp.start()
    loads[0].wait()
    w_wide[...] = w_ref[...].astype(jnp.float32)
    for j in range(8):
        for half in (0, 1):
            w_heads[j, :, half * QT : (half + 1) * QT] = w_wide[pl.ds(2 * j + half, 160, stride=16), :].astype(
                jnp.bfloat16
            )
    for h in (0, 1):
        wx[h, x] = w_heads[x + NX * h]
    loads[1].wait()
    for i in range(NG):
        augx[i, x] = aug_ref[:, i * QT : (i + 1) * QT]
    pl.semaphore_wait(barrier, len(partners))

    w_sends = []
    for i, d in enumerate((1, 2, 3)):
        to_x = wrap(x + d, NX)
        cp = remote(w_heads.at[to_x + NX * c], wx.at[c, x], wx_s.at[i], wx_r.at[i], x_to[i])
        cp.start()
        w_sends.append(cp)
    quarters = [g, wrap(g - 1, NG), wrap(g + 1, NG), wrap(g + 2, NG)]
    a_sends = []
    for j, qt in enumerate(quarters):
        for i in range(3):
            cp = remote(
                augx.at[qt, x],
                augx.at[qt, x],
                ax_s.at[j, i],
                ax_r.at[j, i],
                x_to[i],
            )
            cp.start()
            a_sends.append(cp)
    w_shares = []
    for i, d in enumerate((1, 2, 3)):
        src = wrap(x - d, NX)
        remote(wx.at[c, src], wx.at[c, src], wx_s.at[i], wx_r.at[i], x_to[i]).wait_recv()
        cp = remote(wx.at[c, src], wx.at[c, src], ws_s.at[i], ws_r.at[i], sib)
        cp.start()
        w_shares.append(cp)
    for i, d in enumerate((1, 2, 3)):
        src = wrap(x - d, NX)
        remote(wx.at[1 - c, src], wx.at[1 - c, src], ws_s.at[i], ws_r.at[i], sib).wait_recv()

    def arrive_states(j):
        for i, d in enumerate((1, 2, 3)):
            slot = augx.at[quarters[j], wrap(x - d, NX)]
            remote(slot, slot, ax_s.at[j, i], ax_r.at[j, i], x_to[i]).wait_recv()

    def share(target):
        states = augx[lax.rem(target, NG)].reshape(NX * 160, QT)
        weights = wx[lax.div(target, NG)].reshape(NX * 160, 2 * QT)
        return lax.dot_general(
            states, weights, (((0,), (0,)), ((), ())), preferred_element_type=jnp.float32
        )

    sends = []

    def send_p(k, half):
        cp = remote(op.at[k - 1, half], ip.at[k - 1, half], rp_s.at[k - 1, half], rp_r.at[k - 1, half], z_next)
        cp.start()
        sends.append(cp)

    def send_m(k, half):
        cp = remote(om.at[k - 1, half], im.at[k - 1, half], rm_s.at[k - 1, half], rm_r.at[k - 1, half], z_prev)
        cp.start()
        sends.append(cp)

    def got_p(k, half):
        slot = ip.at[k - 1, half]
        remote(slot, slot, rp_s.at[k - 1, half], rp_r.at[k - 1, half], z_next).wait_recv()
        return ip[k - 1, half]

    def got_m(k, half):
        slot = im.at[k - 1, half]
        remote(slot, slot, rm_s.at[k - 1, half], rm_r.at[k - 1, half], z_prev).wait_recv()
        return im[k - 1, half]

    arrive_states(0)
    part = share(wrap(z + 4, NZ))
    op[3, 0] = part[:, :QT]
    om[3, 1] = part[:, QT:]
    send_p(4, 0)
    send_m(4, 1)
    arrive_states(1)
    part = share(wrap(z + 3, NZ))
    op[2, 1] = part[:, QT:]
    send_p(3, 1)
    op[2, 0] = part[:, :QT]
    arrive_states(2)
    part = share(wrap(z - 3, NZ))
    om[2, 0] = part[:, :QT]
    send_m(3, 0)
    om[2, 1] = part[:, QT:]
    arrive_states(3)
    part = share(wrap(z + 2, NZ))
    op[1, 0] = part[:, :QT]
    op[1, 1] = part[:, QT:]
    part = share(wrap(z - 2, NZ))
    om[1, 0] = part[:, :QT]
    om[1, 1] = part[:, QT:]
    op[2, 0] += got_p(4, 0)
    send_p(3, 0)
    om[2, 1] += got_m(4, 1)
    send_m(3, 1)
    part = share(wrap(z + 1, NZ))
    op[0, 0] = part[:, :QT]
    op[0, 1] = part[:, QT:]
    part = share(wrap(z - 1, NZ))
    om[0, 0] = part[:, :QT]
    om[0, 1] = part[:, QT:]
    own[...] = share(z)
    for k in (3, 2):
        for first in (0, 1):
            hp, hm = 1 - first, first
            op[k - 2, hp] += got_p(k, hp)
            send_p(k - 1, hp)
            om[k - 2, hm] += got_m(k, hm)
            send_m(k - 1, hm)

    low = own[:, :QT] + got_m(1, 0)
    high = own[:, QT:] + got_p(1, 1)
    low += got_p(1, 0)
    high += got_m(1, 1)
    kvs[y, c, g, :, :QT] = low.astype(jnp.bfloat16)
    kvs[y, c, g, :, QT:] = high.astype(jnp.bfloat16)

    def quarter_of_own(e, qt):
        slot = kvs.at[y, c, qt]
        return remote(slot, slot, zg_s.at[e - 1], zg_r.at[e - 1], g_to[e - 1])

    for e in (2, 3, 1):
        cp = quarter_of_own(e, g)
        cp.start()
        sends.append(cp)

    units = (g, g2, g3)

    def ring_p(d, u):
        slot = kvs.at[wrap(y - d, NY), c, units[u]]
        return remote(slot, slot, yp_s.at[d, u], yp_r.at[d, u], y_next)

    def ring_m(d, u):
        slot = kvs.at[wrap(y + d, NY), c, units[u]]
        return remote(slot, slot, ym_s.at[d, u], ym_r.at[d, u], y_prev)

    def arrive_p(d, u):
        slot = kvs.at[wrap(y - d, NY), c, units[u]]
        remote(slot, slot, yp_s.at[d - 1, u], yp_r.at[d - 1, u], y_next).wait_recv()

    def arrive_m(d, u):
        slot = kvs.at[wrap(y + d, NY), c, units[u]]
        remote(slot, slot, ym_s.at[d - 1, u], ym_r.at[d - 1, u], y_prev).wait_recv()

    def swap_p(d, qt):
        slot = kvs.at[wrap(y - d, NY), c, qt]
        return remote(slot, slot, zq_s.at[d - 1], zq_r.at[d - 1], g_to[0])

    def swap_m(d, qt):
        slot = kvs.at[wrap(y + d, NY), c, lax.rem(qt + 2 * lax.div(d, 4), NG)]
        return remote(slot, slot, zq_s.at[3 + d], zq_r.at[3 + d], g_to[0])

    def sibling(yi, ci):
        slot = kvs.at[yi, ci]
        return remote(slot, slot, sb_s.at[yi], sb_r.at[yi], sib)

    for u in range(3):
        if u > 0:
            quarter_of_own(u + 1, units[u]).wait_recv()
        ring_p(0, u).start()
        ring_m(0, u).start()
    quarter_of_own(1, g1).wait_recv()
    sibling(y, c).start()
    loads[2].wait()

    scale = LOG2E * 128 ** -0.5
    scores = (sc0, sc1)

    def score(yi, rb):
        q = q_ref[rb * ROWS : (rb + 1) * ROWS, :]
        block = kvs.at[yi].reshape(8 * QT, 2 * QT)
        for h in range(4):
            scores[rb % 2][:, h * 256 : (h + 1) * 256] = lax.dot_general(
                q, block[h * 256 : (h + 1) * 256, :QT], (((1,), (1,)), ((), ())), preferred_element_type=jnp.float32
            )

    def weigh(yi, rb, diagonal):
        rows = slice(rb * ROWS, (rb + 1) * ROWS)
        block = kvs.at[yi].reshape(8 * QT, 2 * QT)
        qo = order_ref[2 * seq + rb * ROWS // 512]
        s = scores[rb % 2]
        parts = [s[:, i * QT : (i + 1) * QT] for i in range(8)]
        if diagonal:
            row = lax.broadcasted_iota(jnp.int32, (ROWS, QT), 0) + (rb * ROWS) % 512
            ahead = lax.shift_right_logical(row, 1) - lax.broadcasted_iota(jnp.int32, (ROWS, QT), 1)
            for i in range(8):
                ko = order_ref[4 * yi + i // 2]
                parts[i] = jnp.where(ahead >= (ko - qo) * 256 + (i % 2) * QT, parts[i], NEG)
            bias = [None] * 4
        else:
            bias = [jnp.where(order_ref[4 * yi + h] < qo, 0.0, NEG) for h in range(4)]
        top = None
        for h in range(4):
            t = jnp.maximum(parts[2 * h], parts[2 * h + 1])
            t = t if diagonal else t + bias[h]
            top = t if top is None else jnp.maximum(top, t)
        new = jnp.broadcast_to(jnp.max(top, axis=-1, keepdims=True), (ROWS, QT))
        if not diagonal:
            old = m_ref[rows, :]
            new = jnp.maximum(old, new)
        m_ref[rows, :] = new
        total, o = None, None
        for h in range(4):
            base = new if diagonal else new - bias[h]
            pair = [jnp.exp2((parts[2 * h + i] - base) * scale) for i in (0, 1)]
            t = pair[0] + pair[1]
            total = t if total is None else total + t
            probs = jnp.concatenate([v.astype(jnp.bfloat16) for v in pair], axis=1)
            t = jnp.dot(probs, block[h * 256 : (h + 1) * 256, QT:], preferred_element_type=jnp.float32)
            o = t if o is None else o + t
        if diagonal:
            l_ref[rows, :] = total
            acc_ref[rows, :] = o
        else:
            alpha = jnp.exp2((old - new) * scale)
            l_ref[rows, :] = l_ref[rows, :] * alpha + total
            acc_ref[rows, :] = acc_ref[rows, :] * alpha + o

    def first_half(yi, diagonal=False):
        score(yi, 0)
        score(yi, 1)
        weigh(yi, 0, diagonal)
        score(yi, 2)
        weigh(yi, 1, diagonal)

    def second_half(yi, diagonal=False):
        score(yi, 3)
        weigh(yi, 2, diagonal)
        weigh(yi, 3, diagonal)

    def when(cond, do):
        if isinstance(cond, bool):
            if cond:
                do()
        else:
            pl.when(cond)(do)

    def step(d):
        new_p, new_m = wrap(y - d, NY), wrap(y + d, NY)

        def unit(u):
            def plus():
                arrive_p(d, u)
                when(d < 4 if u == 0 else d < 3, lambda: ring_p(d, u).start())
                if u == 0:
                    swap_p(d, g).start()

            def minus():
                arrive_m(d, u)
                when(d < 4 if u == 1 else d < 3, lambda: ring_m(d, u).start())
                if u == 0:
                    swap_m(d, g).start()
                elif u == 1:
                    when(d == 4, lambda: swap_m(d, g).start())

            when(True if u == 0 else d < 4, plus)
            when(True if u == 1 else d < 4, minus)

        def complete():
            swap_p(d, g1).wait_recv()
            swap_m(d, g1).wait_recv()
            sibling(new_p, c).start()
            when(d < 4, lambda: sibling(new_m, c).start())

        return unit, complete

    def wait_sibling(yi):
        sibling(yi, 1 - c).wait_recv()

    unit, complete = step(1)
    wait_sibling(y)
    first_half(y, True)
    unit(0)
    second_half(y, True)
    unit(1)
    unit(2)
    complete()

    def onward(d, carry):
        unit, complete = step(d)
        last_p, last_m = wrap(y - d + 1, NY), wrap(y + d - 1, NY)
        unit(0)
        wait_sibling(last_p)
        first_half(last_p)
        unit(1)
        wait_sibling(last_m)
        second_half(last_p)
        first_half(last_m)
        unit(2)
        complete()
        second_half(last_m)
        return carry

    lax.fori_loop(2, 5, onward, 0)
    far = wrap(y + 4, NY)
    wait_sibling(far)
    first_half(far)
    second_half(far)

    out_ref[...] = (acc_ref[...] / jnp.sum(l_ref[...], axis=-1, keepdims=True)).astype(jnp.bfloat16)

    for cp in w_sends + a_sends + w_shares + sends:
        cp.wait_send()

    def drain(d, carry):
        for u in range(3):
            when(True if u == 0 else d < 3, lambda: ring_p(d, u).wait_send())
            when(True if u == 1 else d < 3, lambda: ring_m(d, u).wait_send())
        swap_p(d + 1, g).wait_send()
        swap_m(d + 1, g).wait_send()
        return carry

    lax.fori_loop(0, 4, drain, 0)

    def drain_sibling(yi, carry):
        sibling(yi, c).wait_send()
        return carry

    lax.fori_loop(0, NY, drain_sibling, 0)


def body(queries, aug_states, key_value_weight, block_order):
    tok = queries.shape[0]
    rows = tok * queries.shape[2]
    q = queries.reshape(rows, 128)
    aug = aug_states.T
    w = key_value_weight.reshape(2560, 128)
    dma = pltpu.SemaphoreType.DMA
    out = pl.pallas_call(
        kernel,
        out_shape=jax.ShapeDtypeStruct((rows, 128), jnp.bfloat16),
        in_specs=[pl.BlockSpec(memory_space=pltpu.SMEM)] + [pl.BlockSpec(memory_space=pltpu.HBM)] * 3,
        out_specs=pl.BlockSpec(memory_space=pltpu.VMEM),
        scratch_shapes=[
            pltpu.VMEM((rows, 128), jnp.bfloat16),
            pltpu.VMEM((160, 512), jnp.bfloat16),
            pltpu.VMEM((2560, 128), jnp.bfloat16),
            pltpu.VMEM((2560, 128), jnp.float32),
            pltpu.VMEM((8, 160, 2 * QT), jnp.bfloat16),
            pltpu.VMEM((NG, NX, 160, QT), jnp.bfloat16),
            pltpu.VMEM((2, NX, 160, 2 * QT), jnp.bfloat16),
            pltpu.VMEM((4, 2, QT, QT), jnp.float32),
            pltpu.VMEM((4, 2, QT, QT), jnp.float32),
            pltpu.VMEM((4, 2, QT, QT), jnp.float32),
            pltpu.VMEM((4, 2, QT, QT), jnp.float32),
            pltpu.VMEM((QT, 2 * QT), jnp.float32),
            pltpu.VMEM((NY, 2, NG, QT, 2 * QT), jnp.bfloat16),
            pltpu.VMEM((rows, 128), jnp.float32),
            pltpu.VMEM((rows, 128), jnp.float32),
            pltpu.VMEM((rows, 128), jnp.float32),
            pltpu.VMEM((ROWS, 8 * QT), jnp.float32),
            pltpu.VMEM((ROWS, 8 * QT), jnp.float32),
            dma((4, 3)),
            dma((4, 3)),
            dma((3,)),
            dma((3,)),
            dma((3,)),
            dma((3,)),
            dma((4, 2)),
            dma((4, 2)),
            dma((4, 2)),
            dma((4, 2)),
            dma((3,)),
            dma((3,)),
            dma((8,)),
            dma((8,)),
            dma((4, 3)),
            dma((4, 3)),
            dma((4, 3)),
            dma((4, 3)),
            dma((8,)),
            dma((8,)),
            dma((6,)),
        ],
        compiler_params=pltpu.CompilerParams(
            collective_id=0, has_side_effects=True, vmem_limit_bytes=62 * 1024 * 1024
        ),
        cost_estimate=pl.CostEstimate(flops=9 * 10**9, bytes_accessed=2 * 10**6, transcendentals=8 * 10**6),
        name="compose",
    )(block_order, q, aug, w)
    return out.reshape(queries.shape)


def solution(mesh):
    in_specs = (
        P("seq", "tp", "group", None),
        P("seq", ("group", "tp")),
        P(("group", "tp"), None, None, None),
        P(),
    )
    out_specs = P("seq", "tp", "group", None)
    return jax.shard_map(body, mesh=mesh, in_specs=in_specs, out_specs=out_specs, check_vma=False)
```

```python
import functools

import jax
import jax.numpy as jnp
from jax import lax
from jax.experimental import pallas as pl
from jax.experimental.pallas import tpu as pltpu
from jax.sharding import PartitionSpec as P

MESH = pl.DeviceIdType.MESH
NX, NY, NZ, NG = 4, 8, 8, 4
QT = 128
ROWS = 256
NEG = -1e30
LOG2E = 1.4426950408889634


def kernel(
    order_ref,
    q_hbm,
    aug_hbm,
    w_hbm,
    out_ref,
    q_ref,
    aug_ref,
    w_ref,
    w_wide,
    w_heads,
    augx,
    wx,
    op,
    om,
    ip,
    im,
    own,
    kvs,
    m_ref,
    l_ref,
    acc_ref,
    sc0,
    sc1,
    out_s,
    ax_r,
    wx_r,
    ws_r,
    rp_r,
    rm_r,
    zg_r,
    zq_r,
    yp_r,
    ym_r,
    far_r,
    sb_r,
    loc,
):
    g = lax.axis_index("group")
    seq = lax.axis_index("seq")
    tp = lax.axis_index("tp")
    y, c = lax.div(seq, 2), lax.rem(seq, 2)
    zh, x = lax.div(tp, NX), lax.rem(tp, NX)
    z = zh * NG + g

    def dev(z=z, y=y, c=c, x=x):
        return (lax.rem(z, NG), y * 2 + c, lax.div(z, NG) * NX + x)

    def remote(src, dst, send, recv, to):
        return pltpu.make_async_remote_copy(
            src_ref=src, dst_ref=dst, send_sem=send, recv_sem=recv, device_id=to, device_id_type=MESH
        )

    def wrap(v, n):
        return lax.rem(v + 4 * n, n)

    x_to = [dev(x=wrap(x + d, NX)) for d in (1, 2, 3)]
    z_next, z_prev = dev(z=wrap(z + 1, NZ)), dev(z=wrap(z - 1, NZ))
    g1, g2, g3 = g + 1 - 2 * lax.rem(g, 2), lax.rem(g + 2, NG), 3 - g
    g_to = [dev(z=zh * NG + v) for v in (g1, g2, g3)]
    y_next, y_prev = dev(y=wrap(y + 1, NY)), dev(y=wrap(y - 1, NY))
    sib = dev(c=1 - c)
    far_next = dev(z=zh * NG + g1, y=wrap(y + 1, NY))
    far_prev = dev(z=zh * NG + g1, y=wrap(y - 1, NY))

    barrier = pltpu.get_barrier_semaphore()
    partners = x_to + [z_next, z_prev] + g_to + [y_next, y_prev, sib, far_next, far_prev]
    for to in partners:
        pl.semaphore_signal(barrier, inc=1, device_id=to, device_id_type=MESH)

    loads = [
        pltpu.make_async_copy(w_hbm, w_ref, loc.at[0]),
        pltpu.make_async_copy(aug_hbm, aug_ref, loc.at[1]),
        pltpu.make_async_copy(q_hbm, q_ref, loc.at[2]),
    ]
    for cp in loads:
        cp.start()
    loads[0].wait()
    w_wide[...] = w_ref[...].astype(jnp.float32)
    for j in range(8):
        for half in (0, 1):
            w_heads[j, :, half * QT : (half + 1) * QT] = w_wide[pl.ds(2 * j + half, 160, stride=16), :].astype(
                jnp.bfloat16
            )
    for h in (0, 1):
        wx[h, x] = w_heads[x + NX * h]
    loads[1].wait()
    for i in range(NG):
        augx[i, x] = aug_ref[:, i * QT : (i + 1) * QT]
    pl.semaphore_wait(barrier, len(partners))

    heads = (1 - zh, zh)
    band = pl.ds(pl.multiple_of(80 * c, 16), 80)

    def send_weights(n):
        for i, d in enumerate((1, 2, 3)):
            src = w_heads.at[wrap(x + d, NX) + NX * heads[n], band]
            remote(src, wx.at[heads[n], x, band], out_s.at[0], wx_r.at[n], x_to[i]).start()

    def arrive_weights(n):
        three = wx.at[0, 0:3, band]
        remote(three, three, out_s.at[0], wx_r.at[n], sib).wait_recv()
        for d in (1, 2, 3):
            slot = wx.at[heads[n], wrap(x - d, NX), band]
            remote(slot, slot, out_s.at[1], ws_r.at[n], sib).start()
        remote(three, three, out_s.at[1], ws_r.at[n], sib).wait_recv()

    quarters = [g, wrap(g - 1, NG), wrap(g + 1, NG), wrap(g + 2, NG)]

    def send_states(j):
        slot = augx.at[quarters[j], x]
        for i in range(3):
            remote(slot, slot, out_s.at[2], ax_r.at[j], x_to[i]).start()

    def arrive_states(j):
        three = augx.at[0, 0:3]
        remote(three, three, out_s.at[2], ax_r.at[j], sib).wait_recv()

    send_weights(0)
    send_states(0)
    send_weights(1)
    for j in (1, 2, 3):
        send_states(j)
    arrive_weights(0)

    def share(target):
        states = augx[lax.rem(target, NG)].reshape(NX * 160, QT)
        weights = wx[lax.div(target, NG)].reshape(NX * 160, 2 * QT)
        return lax.dot_general(
            states, weights, (((0,), (0,)), ((), ())), preferred_element_type=jnp.float32
        )

    def send_p(k, half):
        remote(op.at[k - 1, half], ip.at[k - 1, half], out_s.at[3 + k // 4], rp_r.at[k - 1, half], z_next).start()

    def send_m(k, half):
        remote(om.at[k - 1, half], im.at[k - 1, half], out_s.at[5 + k // 4], rm_r.at[k - 1, half], z_prev).start()

    def got_p(k, half):
        slot = ip.at[k - 1, half]
        remote(slot, slot, out_s.at[3 + k // 4], rp_r.at[k - 1, half], z_next).wait_recv()
        return ip[k - 1, half]

    def got_m(k, half):
        slot = im.at[k - 1, half]
        remote(slot, slot, out_s.at[5 + k // 4], rm_r.at[k - 1, half], z_prev).wait_recv()
        return im[k - 1, half]

    def fill(buf, k, part, halves=(0, 1)):
        for half in halves:
            buf[k - 1, half] = part[:, half * QT : (half + 1) * QT]

    arrive_states(0)
    part = share(wrap(z + 4, NZ))
    fill(op, 4, part, (0,))
    fill(om, 4, part, (1,))
    send_p(4, 0)
    send_m(4, 1)
    arrive_weights(1)
    arrive_states(1)
    fill(op, 3, share(wrap(z + 3, NZ)))
    send_p(3, 1)
    arrive_states(2)
    fill(om, 3, share(wrap(z - 3, NZ)))
    send_m(3, 0)
    op[2, 0] += got_p(4, 0)
    send_p(3, 0)
    om[2, 1] += got_m(4, 1)
    send_m(3, 1)
    arrive_states(3)
    fill(op, 2, share(wrap(z + 2, NZ)))
    fill(om, 2, share(wrap(z - 2, NZ)))
    fill(op, 1, share(wrap(z + 1, NZ)))
    fill(om, 1, share(wrap(z - 1, NZ)))
    own[...] = share(z)
    for k in (3, 2):
        for first in (0, 1):
            hp, hm = 1 - first, first
            op[k - 2, hp] += got_p(k, hp)
            send_p(k - 1, hp)
            om[k - 2, hm] += got_m(k, hm)
            send_m(k - 1, hm)

    low = own[:, :QT] + got_m(1, 0)
    high = own[:, QT:] + got_p(1, 1)
    kvs[0, y, g, c] = (low + got_p(1, 0)).astype(jnp.bfloat16)
    kvs[1, y, g, c] = (high + got_m(1, 1)).astype(jnp.bfloat16)

    def quarter_of_own(e, qt):
        slot = kvs.at[:, y, qt, c]
        return remote(slot, slot, out_s.at[7], zg_r.at[e - 1], g_to[e - 1])

    units = (g, g2, g3)
    far = wrap(y + 4, NY)

    def ring_p(d, u):
        slot = kvs.at[:, wrap(y - d, NY), units[u], c]
        return remote(slot, slot, out_s.at[8], yp_r.at[d, u], y_next)

    def ring_m(d, u):
        slot = kvs.at[:, wrap(y + d, NY), units[u], c]
        return remote(slot, slot, out_s.at[9], ym_r.at[d, u], y_prev)

    def arrive_p(d, u):
        slot = kvs.at[:, wrap(y - d, NY), units[u], c]
        remote(slot, slot, out_s.at[8], yp_r.at[d - 1, u], y_next).wait_recv()

    def arrive_m(d, u):
        slot = kvs.at[:, wrap(y + d, NY), units[u], c]
        remote(slot, slot, out_s.at[9], ym_r.at[d - 1, u], y_prev).wait_recv()

    def swap(yi, d):
        slot = kvs.at[:, yi, g, c]
        remote(slot, slot, out_s.at[10], zq_r.at[d - 1], g_to[0]).start()

    def far_p(qt):
        slot = kvs.at[:, wrap(y - 3, NY), qt, c]
        return remote(slot, slot, out_s.at[11], far_r.at[0], far_next)

    def far_m(qt):
        slot = kvs.at[:, wrap(y + 3, NY), qt, c]
        return remote(slot, slot, out_s.at[11], far_r.at[1], far_prev)

    def share_core(group, yi, qt):
        slot = kvs.at[:, yi, qt, c]
        remote(slot, slot, out_s.at[12], sb_r.at[group], sib).start()

    def from_sibling(group):
        four = kvs.at[:, 0:2, 0:2, 0]
        remote(four, four, out_s.at[12], sb_r.at[group], sib).wait_recv()

    def own_unit(u):
        quarter_of_own(u + 1, units[u]).wait_recv()
        ring_p(0, u).start()
        ring_m(0, u).start()
        share_core(0, y, units[u])

    ring_p(0, 0).start()
    ring_m(0, 0).start()
    for e in (2, 3, 1):
        quarter_of_own(e, g).start()
    share_core(0, y, g)
    loads[2].wait()

    scale = LOG2E * 128 ** -0.5
    scores = (sc0, sc1)

    def score(pairs, rb, s):
        q = q_ref[rb * ROWS : (rb + 1) * ROWS, :]
        for h, (yi, qt) in enumerate(pairs):
            keys = kvs[0, yi, qt].reshape(2 * QT, QT)
            s[:, h * 256 : (h + 1) * 256] = lax.dot_general(
                q, keys, (((1,), (1,)), ((), ())), preferred_element_type=jnp.float32
            )

    def weigh(pairs, rb, s, diagonal):
        rows = slice(rb * ROWS, (rb + 1) * ROWS)
        n = len(pairs)
        qo = order_ref[2 * seq + rb * ROWS // 512]
        parts = [s[:, i * QT : (i + 1) * QT] for i in range(2 * n)]
        places = [order_ref[4 * yi + 2 * ci + lax.div(qt, 2)] for yi, qt in pairs for ci in (0, 1)]
        if diagonal:
            row = lax.broadcasted_iota(jnp.int32, (ROWS, QT), 0) + (rb * ROWS) % 512
            ahead = lax.shift_right_logical(row, 1) - lax.broadcasted_iota(jnp.int32, (ROWS, QT), 1)
            for i in range(2 * n):
                start = (places[i] - qo) * 256 + lax.rem(pairs[i // 2][1], 2) * QT
                parts[i] = jnp.where(ahead >= start, parts[i], NEG)
            tops = parts
        else:
            bias = [jnp.where(place < qo, 0.0, NEG) for place in places]
            tops = [parts[i] + bias[i] for i in range(2 * n)]
        top = functools.reduce(jnp.maximum, tops)
        new = jnp.broadcast_to(jnp.max(top, axis=-1, keepdims=True), (ROWS, QT))
        if not diagonal:
            old = m_ref[rows, :]
            new = jnp.maximum(old, new)
        m_ref[rows, :] = new
        total, o = None, None
        for h, (yi, qt) in enumerate(pairs):
            pair = []
            for i in (2 * h, 2 * h + 1):
                base = new if diagonal else new - bias[i]
                pair.append(jnp.exp2((parts[i] - base) * scale))
            t = pair[0] + pair[1]
            total = t if total is None else total + t
            probs = jnp.concatenate([v.astype(jnp.bfloat16) for v in pair], axis=1)
            values = kvs[1, yi, qt].reshape(2 * QT, QT)
            t = jnp.dot(probs, values, preferred_element_type=jnp.float32)
            o = t if o is None else o + t
        if diagonal:
            l_ref[rows, :] = total
            acc_ref[rows, :] = o
        else:
            alpha = jnp.exp2((old - new) * scale)
            l_ref[rows, :] = l_ref[rows, :] * alpha + total
            acc_ref[rows, :] = acc_ref[rows, :] * alpha + o

    def pairs_of(d, first):
        behind, before = wrap(y - d, NY), wrap(y + d, NY)
        return [(yi, qt) for qt in ((g, g2) if first else (g3, g1)) for yi in (behind, before)]

    chunks = [[(y, qt) for qt in range(NG)]]
    for d in (1, 2, 3):
        chunks += [pairs_of(d, True), pairs_of(d, False)]
    chunks.append([(far, qt) for qt in (g, g1, g2, g3)])
    state = {"next": 0, "scored": 0, "ready": 0}

    def ready(group):
        from_sibling(group)
        state["ready"] += 4

    def work(count):
        for _ in range(count):
            k = state["next"]
            while state["scored"] < min(k + 2, state["ready"]):
                n = state["scored"]
                score(chunks[n // 4], n % 4, scores[n % 2])
                state["scored"] += 1
            weigh(chunks[k // 4], k % 4, scores[k % 2], k < 4)
            state["next"] += 1

    def unit(d, u):
        new_p, new_m = wrap(y - d, NY), wrap(y + d, NY)
        group = 2 * d - (1 if u < 2 else 0)
        arrive_p(d, u)
        if d < 3 or u == 0:
            ring_p(d, u).start()
        if u == 0:
            if d == 3:
                far_p(g).start()
            swap(new_p, d)
        share_core(group, new_p, units[u])
        arrive_m(d, u)
        if d < 3 or u == 1:
            ring_m(d, u).start()
        if u == 1 and d == 3:
            far_m(g2).start()
        if u == 0:
            swap(new_m, d)
        share_core(group, new_m, units[u])

    def swapped(d):
        two = kvs.at[:, y, 0:2, c]
        remote(two, two, out_s.at[10], zq_r.at[d - 1], sib).wait_recv()
        share_core(2 * d, wrap(y - d, NY), g1)
        share_core(2 * d, wrap(y + d, NY), g1)

    own_unit(1)
    unit(1, 0)
    own_unit(2)
    quarter_of_own(1, g1).wait_recv()
    share_core(0, y, g1)
    ready(0)
    work(2)
    unit(2, 0)
    unit(1, 1)
    work(1)
    swapped(1)
    unit(1, 2)
    work(1)
    ready(1)
    work(2)
    unit(3, 0)
    work(1)
    unit(2, 1)
    swapped(2)
    ready(2)
    work(2)
    unit(2, 2)
    work(3)
    arrive_p(4, 0)
    share_core(7, far, g)
    ready(3)
    work(1)
    unit(3, 1)
    swapped(3)
    work(2)
    unit(3, 2)
    ready(4)
    work(4)
    arrive_m(4, 1)
    share_core(7, far, g2)
    ready(5)
    work(4)
    for i, qt in ((0, g1), (1, g3)):
        slot = kvs.at[:, far, qt, c]
        remote(slot, slot, out_s.at[11], far_r.at[i], sib).wait_recv()
        share_core(7, far, qt)
    ready(6)
    work(3)
    ready(7)
    work(len(chunks) * 4 - state["next"])

    out_ref[...] = (acc_ref[...] / jnp.sum(l_ref[...], axis=-1, keepdims=True)).astype(jnp.bfloat16)

    sent = [
        w_heads.at[0:3],
        w_heads.at[0:3],
        augx.at[0:3],
        op.at[0:3],
        op.at[3, 0],
        om.at[0:3],
        om.at[3, 1],
        kvs.at[:, 0, 0:3, 0],
        kvs.at[:, 0:5, 0:2, 0],
        kvs.at[:, 0:5, 0:2, 0],
        kvs.at[:, 0:3, 0:2, 0],
        kvs.at[:, 0, 0:2, 0],
        kvs.at[:, :, :, 0],
    ]
    for i, ref in enumerate(sent):
        remote(ref, ref, out_s.at[i], far_r.at[0], sib).wait_send()


def body(queries, aug_states, key_value_weight, block_order):
    tok = queries.shape[0]
    rows = tok * queries.shape[2]
    q = queries.reshape(rows, 128)
    aug = aug_states.T
    w = key_value_weight.reshape(2560, 128)
    dma = pltpu.SemaphoreType.DMA
    out = pl.pallas_call(
        kernel,
        out_shape=jax.ShapeDtypeStruct((rows, 128), jnp.bfloat16),
        in_specs=[pl.BlockSpec(memory_space=pltpu.SMEM)] + [pl.BlockSpec(memory_space=pltpu.HBM)] * 3,
        out_specs=pl.BlockSpec(memory_space=pltpu.VMEM),
        scratch_shapes=[
            pltpu.VMEM((rows, 128), jnp.bfloat16),
            pltpu.VMEM((160, 512), jnp.bfloat16),
            pltpu.VMEM((2560, 128), jnp.bfloat16),
            pltpu.VMEM((2560, 128), jnp.float32),
            pltpu.VMEM((8, 160, 2 * QT), jnp.bfloat16),
            pltpu.VMEM((NG, NX, 160, QT), jnp.bfloat16),
            pltpu.VMEM((2, NX, 160, 2 * QT), jnp.bfloat16),
            pltpu.VMEM((4, 2, QT, QT), jnp.float32),
            pltpu.VMEM((4, 2, QT, QT), jnp.float32),
            pltpu.VMEM((4, 2, QT, QT), jnp.float32),
            pltpu.VMEM((4, 2, QT, QT), jnp.float32),
            pltpu.VMEM((QT, 2 * QT), jnp.float32),
            pltpu.VMEM((2, NY, NG, 2, QT, QT), jnp.bfloat16),
            pltpu.VMEM((rows, 128), jnp.float32),
            pltpu.VMEM((rows, 128), jnp.float32),
            pltpu.VMEM((rows, 128), jnp.float32),
            pltpu.VMEM((ROWS, 8 * QT), jnp.float32),
            pltpu.VMEM((ROWS, 8 * QT), jnp.float32),
            dma((13,)),
            dma((4,)),
            dma((2,)),
            dma((2,)),
            dma((4, 2)),
            dma((4, 2)),
            dma((3,)),
            dma((3,)),
            dma((4, 3)),
            dma((4, 3)),
            dma((2,)),
            dma((8,)),
            dma((3,)),
        ],
        compiler_params=pltpu.CompilerParams(
            collective_id=0, has_side_effects=True, vmem_limit_bytes=62 * 1024 * 1024
        ),
        cost_estimate=pl.CostEstimate(flops=9 * 10**9, bytes_accessed=2 * 10**6, transcendentals=8 * 10**6),
        name="compose",
    )(block_order, q, aug, w)
    return out.reshape(queries.shape)


def solution(mesh):
    in_specs = (
        P("seq", "tp", "group", None),
        P("seq", ("group", "tp")),
        P(("group", "tp"), None, None, None),
        P(),
    )
    out_specs = P("seq", "tp", "group", None)
    return jax.shard_map(body, mesh=mesh, in_specs=in_specs, out_specs=out_specs, check_vma=False)
```

```python
import functools

import jax
import jax.numpy as jnp
from jax import lax
from jax.experimental import pallas as pl
from jax.experimental.pallas import tpu as pltpu
from jax.sharding import PartitionSpec as P

MESH = pl.DeviceIdType.MESH
NX, NY, NZ, NG = 4, 8, 8, 4
QT = 128
HALF = 64
ROWS = 256
NEG = -1e30
LOG2E = 1.4426950408889634


def kernel(
    order_ref,
    q_hbm,
    aug_hbm,
    w_hbm,
    out_ref,
    q_ref,
    aug_ref,
    w_ref,
    w_wide,
    w_heads,
    augx,
    wx,
    op,
    om,
    ip,
    im,
    own,
    kvs,
    m_ref,
    l_ref,
    acc_ref,
    sc0,
    sc1,
    out_s,
    ax_r,
    wx_r,
    ws_r,
    rp_r,
    rm_r,
    zg_r,
    zq_r,
    yp_r,
    ym_r,
    far_r,
    sb_r,
    loc,
):
    g = lax.axis_index("group")
    seq = lax.axis_index("seq")
    tp = lax.axis_index("tp")
    y, c = lax.div(seq, 2), lax.rem(seq, 2)
    zh, x = lax.div(tp, NX), lax.rem(tp, NX)
    z = zh * NG + g

    def dev(z=z, y=y, c=c, x=x):
        return (lax.rem(z, NG), y * 2 + c, lax.div(z, NG) * NX + x)

    def remote(src, dst, send, recv, to):
        return pltpu.make_async_remote_copy(
            src_ref=src, dst_ref=dst, send_sem=send, recv_sem=recv, device_id=to, device_id_type=MESH
        )

    def wrap(v, n):
        return lax.rem(v + 4 * n, n)

    x_to = [dev(x=wrap(x + d, NX)) for d in (1, 2, 3)]
    z_next, z_prev = dev(z=wrap(z + 1, NZ)), dev(z=wrap(z - 1, NZ))
    g1, g2, g3 = g + 1 - 2 * lax.rem(g, 2), lax.rem(g + 2, NG), 3 - g
    g_to = [dev(z=zh * NG + v) for v in (g1, g2, g3)]
    y_next, y_prev = dev(y=wrap(y + 1, NY)), dev(y=wrap(y - 1, NY))
    sib = dev(c=1 - c)
    far_next = dev(z=zh * NG + g1, y=wrap(y + 1, NY))
    far_prev = dev(z=zh * NG + g1, y=wrap(y - 1, NY))

    barrier = pltpu.get_barrier_semaphore()
    partners = x_to + [z_next, z_prev] + g_to + [y_next, y_prev, sib, far_next, far_prev]
    for to in partners:
        pl.semaphore_signal(barrier, inc=1, device_id=to, device_id_type=MESH)

    loads = [
        pltpu.make_async_copy(w_hbm, w_ref, loc.at[0]),
        pltpu.make_async_copy(aug_hbm, aug_ref, loc.at[1]),
        pltpu.make_async_copy(q_hbm, q_ref, loc.at[2]),
    ]
    for cp in loads:
        cp.start()
    loads[0].wait()
    w_wide[...] = w_ref[...].astype(jnp.float32)
    for j in range(8):
        for half in (0, 1):
            w_heads[j, :, half * QT : (half + 1) * QT] = w_wide[pl.ds(2 * j + half, 160, stride=16), :].astype(
                jnp.bfloat16
            )
    for h in (0, 1):
        wx[h, x] = w_heads[x + NX * h]
    loads[1].wait()
    for i in range(NG):
        augx[i, x] = aug_ref[:, i * QT : (i + 1) * QT]
    pl.semaphore_wait(barrier, len(partners))

    heads = (1 - zh, zh)
    band = pl.ds(pl.multiple_of(80 * c, 16), 80)

    def send_weights(n):
        for i, d in enumerate((1, 2, 3)):
            src = w_heads.at[wrap(x + d, NX) + NX * heads[n], band]
            remote(src, wx.at[heads[n], x, band], out_s.at[0], wx_r.at[n], x_to[i]).start()

    def arrive_weights(n):
        three = wx.at[0, 0:3, band]
        remote(three, three, out_s.at[0], wx_r.at[n], sib).wait_recv()
        for d in (1, 2, 3):
            slot = wx.at[heads[n], wrap(x - d, NX), band]
            remote(slot, slot, out_s.at[1], ws_r.at[n], sib).start()
        remote(three, three, out_s.at[1], ws_r.at[n], sib).wait_recv()

    quarters = [g, wrap(g - 1, NG), wrap(g + 1, NG), wrap(g + 2, NG)]

    def send_states(j):
        slot = augx.at[quarters[j], x]
        for i in range(3):
            remote(slot, slot, out_s.at[2], ax_r.at[j], x_to[i]).start()

    def arrive_states(j):
        three = augx.at[0, 0:3]
        remote(three, three, out_s.at[2], ax_r.at[j], sib).wait_recv()

    send_weights(0)
    send_states(0)
    send_weights(1)
    for j in (1, 2, 3):
        send_states(j)
    arrive_weights(0)

    def share(target):
        states = augx[lax.rem(target, NG)].reshape(NX * 160, QT)
        weights = wx[lax.div(target, NG)].reshape(NX * 160, 2 * QT)
        return lax.dot_general(
            states, weights, (((0,), (0,)), ((), ())), preferred_element_type=jnp.float32
        )

    def send_p(k, kind, r):
        at = (k - 1, kind, r)
        remote(op.at[at], ip.at[at], out_s.at[3 + k // 4], rp_r.at[at], z_next).start()

    def send_m(k, kind, r):
        at = (k - 1, kind, r)
        remote(om.at[at], im.at[at], out_s.at[5 + k // 4], rm_r.at[at], z_prev).start()

    def got_p(k, kind, r):
        at = (k - 1, kind, r)
        remote(ip.at[at], ip.at[at], out_s.at[3 + k // 4], rp_r.at[at], z_next).wait_recv()
        return ip[at]

    def got_m(k, kind, r):
        at = (k - 1, kind, r)
        remote(im.at[at], im.at[at], out_s.at[5 + k // 4], rm_r.at[at], z_prev).wait_recv()
        return im[at]

    def fill(buf, k, part, halves=(0, 1)):
        for kind in (0, 1):
            for r in halves:
                buf[k - 1, kind, r] = part[r * HALF : (r + 1) * HALF, kind * QT : (kind + 1) * QT]

    arrive_states(0)
    part = share(wrap(z + 4, NZ))
    fill(op, 4, part, (0,))
    fill(om, 4, part, (1,))
    for kind in (0, 1):
        send_p(4, kind, 0)
        send_m(4, kind, 1)
    arrive_weights(1)
    arrive_states(1)
    fill(op, 3, share(wrap(z + 3, NZ)))
    for kind in (0, 1):
        send_p(3, kind, 1)
    arrive_states(2)
    fill(om, 3, share(wrap(z - 3, NZ)))
    for kind in (0, 1):
        send_m(3, kind, 0)
    for kind in (0, 1):
        op[2, kind, 0] += got_p(4, kind, 0)
        send_p(3, kind, 0)
        om[2, kind, 1] += got_m(4, kind, 1)
        send_m(3, kind, 1)
    arrive_states(3)
    fill(op, 2, share(wrap(z + 2, NZ)))
    fill(om, 2, share(wrap(z - 2, NZ)))
    fill(op, 1, share(wrap(z + 1, NZ)))
    fill(om, 1, share(wrap(z - 1, NZ)))
    own[...] = share(z)
    for k in (3, 2):
        for kind in (0, 1):
            for first in (0, 1):
                rp, rm = 1 - first, first
                op[k - 2, kind, rp] += got_p(k, kind, rp)
                send_p(k - 1, kind, rp)
                om[k - 2, kind, rm] += got_m(k, kind, rm)
                send_m(k - 1, kind, rm)

    def finish(kind):
        for r in (0, 1):
            rows = slice(r * HALF, (r + 1) * HALF)
            total = own[rows, kind * QT : (kind + 1) * QT] + got_m(1, kind, r) + got_p(1, kind, r)
            kvs[y, g, c, kind, rows] = total.astype(jnp.bfloat16)

    def quarter_of_own(e, qt):
        slot = kvs.at[y, qt, c]
        return remote(slot, slot, out_s.at[7], zg_r.at[e - 1], g_to[e - 1])

    units = (g, g2, g3)
    far = wrap(y + 4, NY)

    def ring_p(d, u):
        slot = kvs.at[wrap(y - d, NY), units[u], c]
        return remote(slot, slot, out_s.at[8], yp_r.at[d, u], y_next)

    def ring_m(d, u):
        slot = kvs.at[wrap(y + d, NY), units[u], c]
        return remote(slot, slot, out_s.at[9], ym_r.at[d, u], y_prev)

    def arrive_p(d, u):
        slot = kvs.at[wrap(y - d, NY), units[u], c]
        remote(slot, slot, out_s.at[8], yp_r.at[d - 1, u], y_next).wait_recv()

    def arrive_m(d, u):
        slot = kvs.at[wrap(y + d, NY), units[u], c]
        remote(slot, slot, out_s.at[9], ym_r.at[d - 1, u], y_prev).wait_recv()

    def swap(yi, d):
        slot = kvs.at[yi, g, c]
        remote(slot, slot, out_s.at[10], zq_r.at[d - 1], g_to[0]).start()

    def far_p(qt):
        slot = kvs.at[wrap(y - 3, NY), qt, c]
        return remote(slot, slot, out_s.at[11], far_r.at[0], far_next)

    def far_m(qt):
        slot = kvs.at[wrap(y + 3, NY), qt, c]
        return remote(slot, slot, out_s.at[11], far_r.at[1], far_prev)

    def share_core(group, yi, qt):
        slot = kvs.at[yi, qt, c]
        remote(slot, slot, out_s.at[12], sb_r.at[group], sib).start()

    def from_sibling(group):
        four = kvs.at[0, :, 0]
        remote(four, four, out_s.at[12], sb_r.at[group], sib).wait_recv()

    def own_unit(u):
        quarter_of_own(u + 1, units[u]).wait_recv()
        ring_p(0, u).start()
        ring_m(0, u).start()
        share_core(0, y, units[u])

    for kind in (0, 1):
        finish(kind)
        slot = kvs.at[y, g, c, kind]
        remote(slot, slot, out_s.at[8], yp_r.at[0, 0], y_next).start()
        remote(slot, slot, out_s.at[9], ym_r.at[0, 0], y_prev).start()
        for e in (2, 3, 1):
            remote(slot, slot, out_s.at[7], zg_r.at[e - 1], g_to[e - 1]).start()
    share_core(0, y, g)
    loads[2].wait()

    scale = LOG2E * 128 ** -0.5
    scores = (sc0, sc1)

    def score(pairs, rb, s):
        q = q_ref[rb * ROWS : (rb + 1) * ROWS, :]
        for h, (yi, qt) in enumerate(pairs):
            keys = jnp.concatenate([kvs[yi, qt, 0, 0], kvs[yi, qt, 1, 0]], axis=0)
            s[:, h * 256 : (h + 1) * 256] = lax.dot_general(
                q, keys, (((1,), (1,)), ((), ())), preferred_element_type=jnp.float32
            )

    def weigh(pairs, rb, s, diagonal):
        rows = slice(rb * ROWS, (rb + 1) * ROWS)
        n = len(pairs)
        qo = order_ref[2 * seq + rb * ROWS // 512]
        parts = [s[:, i * QT : (i + 1) * QT] for i in range(2 * n)]
        places = [order_ref[4 * yi + 2 * ci + lax.div(qt, 2)] for yi, qt in pairs for ci in (0, 1)]
        if diagonal:
            row = lax.broadcasted_iota(jnp.int32, (ROWS, QT), 0) + (rb * ROWS) % 512
            ahead = lax.shift_right_logical(row, 1) - lax.broadcasted_iota(jnp.int32, (ROWS, QT), 1)
            for i in range(2 * n):
                start = (places[i] - qo) * 256 + lax.rem(pairs[i // 2][1], 2) * QT
                parts[i] = jnp.where(ahead >= start, parts[i], NEG)
            tops = parts
        else:
            bias = [jnp.where(place < qo, 0.0, NEG) for place in places]
            tops = [parts[i] + bias[i] for i in range(2 * n)]
        top = functools.reduce(jnp.maximum, tops)
        new = jnp.broadcast_to(jnp.max(top, axis=-1, keepdims=True), (ROWS, QT))
        if not diagonal:
            old = m_ref[rows, :]
            new = jnp.maximum(old, new)
        m_ref[rows, :] = new
        total, o = None, None
        for h, (yi, qt) in enumerate(pairs):
            pair = []
            for i in (2 * h, 2 * h + 1):
                base = new if diagonal else new - bias[i]
                pair.append(jnp.exp2((parts[i] - base) * scale))
            t = pair[0] + pair[1]
            total = t if total is None else total + t
            probs = jnp.concatenate([v.astype(jnp.bfloat16) for v in pair], axis=1)
            values = jnp.concatenate([kvs[yi, qt, 0, 1], kvs[yi, qt, 1, 1]], axis=0)
            t = jnp.dot(probs, values, preferred_element_type=jnp.float32)
            o = t if o is None else o + t
        if diagonal:
            l_ref[rows, :] = total
            acc_ref[rows, :] = o
        else:
            alpha = jnp.exp2((old - new) * scale)
            l_ref[rows, :] = l_ref[rows, :] * alpha + total
            acc_ref[rows, :] = acc_ref[rows, :] * alpha + o

    def pairs_of(d, first):
        behind, before = wrap(y - d, NY), wrap(y + d, NY)
        return [(yi, qt) for qt in ((g, g2) if first else (g3, g1)) for yi in (behind, before)]

    chunks = [[(y, qt) for qt in range(NG)]]
    for d in (1, 2, 3):
        chunks += [pairs_of(d, True), pairs_of(d, False)]
    chunks.append([(far, qt) for qt in (g, g1, g2, g3)])
    state = {"next": 0, "scored": 0, "ready": 0}

    def ready(group):
        from_sibling(group)
        state["ready"] += 4

    def work(count):
        for _ in range(count):
            k = state["next"]
            while state["scored"] < min(k + 2, state["ready"]):
                n = state["scored"]
                score(chunks[n // 4], n % 4, scores[n % 2])
                state["scored"] += 1
            weigh(chunks[k // 4], k % 4, scores[k % 2], k < 4)
            state["next"] += 1

    def unit(d, u):
        new_p, new_m = wrap(y - d, NY), wrap(y + d, NY)
        group = 2 * d - (1 if u < 2 else 0)
        arrive_p(d, u)
        if d < 3 or u == 0:
            ring_p(d, u).start()
        if u == 0:
            if d == 3:
                far_p(g).start()
            swap(new_p, d)
        share_core(group, new_p, units[u])
        arrive_m(d, u)
        if d < 3 or u == 1:
            ring_m(d, u).start()
        if u == 1 and d == 3:
            far_m(g2).start()
        if u == 0:
            swap(new_m, d)
        share_core(group, new_m, units[u])

    def swapped(d):
        two = kvs.at[y, 0:2, c]
        remote(two, two, out_s.at[10], zq_r.at[d - 1], sib).wait_recv()
        share_core(2 * d, wrap(y - d, NY), g1)
        share_core(2 * d, wrap(y + d, NY), g1)

    own_unit(1)
    unit(1, 0)
    own_unit(2)
    quarter_of_own(1, g1).wait_recv()
    share_core(0, y, g1)
    ready(0)
    work(2)
    unit(2, 0)
    unit(1, 1)
    work(1)
    swapped(1)
    unit(1, 2)
    work(1)
    ready(1)
    work(2)
    unit(3, 0)
    work(1)
    unit(2, 1)
    swapped(2)
    ready(2)
    work(2)
    unit(2, 2)
    work(3)
    arrive_p(4, 0)
    share_core(7, far, g)
    ready(3)
    work(1)
    unit(3, 1)
    swapped(3)
    work(2)
    unit(3, 2)
    ready(4)
    work(4)
    arrive_m(4, 1)
    share_core(7, far, g2)
    ready(5)
    work(4)
    for i, qt in ((0, g1), (1, g3)):
        slot = kvs.at[far, qt, c]
        remote(slot, slot, out_s.at[11], far_r.at[i], sib).wait_recv()
        share_core(7, far, qt)
    ready(6)
    work(3)
    ready(7)
    work(len(chunks) * 4 - state["next"])

    out_ref[...] = (acc_ref[...] / jnp.sum(l_ref[...], axis=-1, keepdims=True)).astype(jnp.bfloat16)

    sent = [
        w_heads.at[0:3],
        w_heads.at[0:3],
        augx.at[0:3],
        op.at[0:3],
        op.at[3, :, 0],
        om.at[0:3],
        om.at[3, :, 1],
        kvs.at[0, 0:3, 0],
        kvs.at[0:5, 0:2, 0],
        kvs.at[0:5, 0:2, 0],
        kvs.at[0:3, 0:2, 0],
        kvs.at[0, 0:2, 0],
        kvs.at[:, :, 0],
    ]
    for i, ref in enumerate(sent):
        remote(ref, ref, out_s.at[i], far_r.at[0], sib).wait_send()


def body(queries, aug_states, key_value_weight, block_order):
    tok = queries.shape[0]
    rows = tok * queries.shape[2]
    q = queries.reshape(rows, 128)
    aug = aug_states.T
    w = key_value_weight.reshape(2560, 128)
    dma = pltpu.SemaphoreType.DMA
    out = pl.pallas_call(
        kernel,
        out_shape=jax.ShapeDtypeStruct((rows, 128), jnp.bfloat16),
        in_specs=[pl.BlockSpec(memory_space=pltpu.SMEM)] + [pl.BlockSpec(memory_space=pltpu.HBM)] * 3,
        out_specs=pl.BlockSpec(memory_space=pltpu.VMEM),
        scratch_shapes=[
            pltpu.VMEM((rows, 128), jnp.bfloat16),
            pltpu.VMEM((160, 512), jnp.bfloat16),
            pltpu.VMEM((2560, 128), jnp.bfloat16),
            pltpu.VMEM((2560, 128), jnp.float32),
            pltpu.VMEM((8, 160, 2 * QT), jnp.bfloat16),
            pltpu.VMEM((NG, NX, 160, QT), jnp.bfloat16),
            pltpu.VMEM((2, NX, 160, 2 * QT), jnp.bfloat16),
            pltpu.VMEM((4, 2, 2, HALF, QT), jnp.float32),
            pltpu.VMEM((4, 2, 2, HALF, QT), jnp.float32),
            pltpu.VMEM((4, 2, 2, HALF, QT), jnp.float32),
            pltpu.VMEM((4, 2, 2, HALF, QT), jnp.float32),
            pltpu.VMEM((QT, 2 * QT), jnp.float32),
            pltpu.VMEM((NY, NG, 2, 2, QT, QT), jnp.bfloat16),
            pltpu.VMEM((rows, 128), jnp.float32),
            pltpu.VMEM((rows, 128), jnp.float32),
            pltpu.VMEM((rows, 128), jnp.float32),
            pltpu.VMEM((ROWS, 8 * QT), jnp.float32),
            pltpu.VMEM((ROWS, 8 * QT), jnp.float32),
            dma((13,)),
            dma((4,)),
            dma((2,)),
            dma((2,)),
            dma((4, 2, 2)),
            dma((4, 2, 2)),
            dma((3,)),
            dma((3,)),
            dma((4, 3)),
            dma((4, 3)),
            dma((2,)),
            dma((8,)),
            dma((3,)),
        ],
        compiler_params=pltpu.CompilerParams(
            collective_id=0, has_side_effects=True, vmem_limit_bytes=62 * 1024 * 1024
        ),
        cost_estimate=pl.CostEstimate(flops=9 * 10**9, bytes_accessed=2 * 10**6, transcendentals=8 * 10**6),
        name="compose",
    )(block_order, q, aug, w)
    return out.reshape(queries.shape)


def solution(mesh):
    in_specs = (
        P("seq", "tp", "group", None),
        P("seq", ("group", "tp")),
        P(("group", "tp"), None, None, None),
        P(),
    )
    out_specs = P("seq", "tp", "group", None)
    return jax.shard_map(body, mesh=mesh, in_specs=in_specs, out_specs=out_specs, check_vma=False)
```

```python
import functools

import jax
import jax.numpy as jnp
from jax import lax
from jax.experimental import pallas as pl
from jax.experimental.pallas import tpu as pltpu
from jax.sharding import PartitionSpec as P

MESH = pl.DeviceIdType.MESH
NX, NY, NZ, NG = 4, 8, 8, 4
QT = 128
HALF = 64
ROWS = 256
NEG = -1e30
LOG2E = 1.4426950408889634


def kernel(
    order_ref,
    q_hbm,
    aug_hbm,
    w_hbm,
    out_ref,
    q_ref,
    aug_ref,
    w_ref,
    w_wide,
    w_heads,
    augx,
    wx,
    op,
    om,
    ip,
    im,
    own,
    kvs,
    m_ref,
    l_ref,
    acc_ref,
    sc0,
    sc1,
    out_s,
    ax_r,
    wx_r,
    ws_r,
    rp_r,
    rm_r,
    zg_r,
    zq_r,
    yp_r,
    ym_r,
    far_r,
    sb_r,
    loc,
):
    g = lax.axis_index("group")
    seq = lax.axis_index("seq")
    tp = lax.axis_index("tp")
    y, c = lax.div(seq, 2), lax.rem(seq, 2)
    zh, x = lax.div(tp, NX), lax.rem(tp, NX)
    z = zh * NG + g

    def dev(z=z, y=y, c=c, x=x):
        return (lax.rem(z, NG), y * 2 + c, lax.div(z, NG) * NX + x)

    def remote(src, dst, send, recv, to):
        return pltpu.make_async_remote_copy(
            src_ref=src, dst_ref=dst, send_sem=send, recv_sem=recv, device_id=to, device_id_type=MESH
        )

    def wrap(v, n):
        return lax.rem(v + 4 * n, n)

    x_to = [dev(x=wrap(x + d, NX)) for d in (1, 2, 3)]
    z_next, z_prev = dev(z=wrap(z + 1, NZ)), dev(z=wrap(z - 1, NZ))
    g1, g2, g3 = g + 1 - 2 * lax.rem(g, 2), lax.rem(g + 2, NG), 3 - g
    g_to = [dev(z=zh * NG + v) for v in (g1, g2, g3)]
    y_next, y_prev = dev(y=wrap(y + 1, NY)), dev(y=wrap(y - 1, NY))
    sib = dev(c=1 - c)
    across = dev(y=wrap(y + 4, NY))

    barrier = pltpu.get_barrier_semaphore()
    partners = x_to + [z_next, z_prev] + g_to + [y_next, y_prev, sib, across]
    for to in partners:
        pl.semaphore_signal(barrier, inc=1, device_id=to, device_id_type=MESH)

    loads = [
        pltpu.make_async_copy(w_hbm, w_ref, loc.at[0]),
        pltpu.make_async_copy(aug_hbm, aug_ref, loc.at[1]),
        pltpu.make_async_copy(q_hbm, q_ref, loc.at[2]),
    ]
    for cp in loads:
        cp.start()
    loads[0].wait()
    w_wide[...] = w_ref[...].astype(jnp.float32)
    for j in range(8):
        for half in (0, 1):
            w_heads[j, :, half * QT : (half + 1) * QT] = w_wide[pl.ds(2 * j + half, 160, stride=16), :].astype(
                jnp.bfloat16
            )
    for h in (0, 1):
        wx[h, x] = w_heads[x + NX * h]
    loads[1].wait()
    for i in range(NG):
        augx[i, x] = aug_ref[:, i * QT : (i + 1) * QT]
    pl.semaphore_wait(barrier, len(partners))

    heads = (1 - zh, zh)
    band = pl.ds(pl.multiple_of(80 * c, 16), 80)

    def send_weights(n):
        for i, d in enumerate((1, 2, 3)):
            src = w_heads.at[wrap(x + d, NX) + NX * heads[n], band]
            remote(src, wx.at[heads[n], x, band], out_s.at[0], wx_r.at[n], x_to[i]).start()

    def arrive_weights(n):
        three = wx.at[0, 0:3, band]
        remote(three, three, out_s.at[0], wx_r.at[n], sib).wait_recv()
        for d in (1, 2, 3):
            slot = wx.at[heads[n], wrap(x - d, NX), band]
            remote(slot, slot, out_s.at[1], ws_r.at[n], sib).start()
        remote(three, three, out_s.at[1], ws_r.at[n], sib).wait_recv()

    quarters = [g, wrap(g - 1, NG), wrap(g + 1, NG), wrap(g + 2, NG)]

    def send_states(j):
        slot = augx.at[quarters[j], x]
        for i in range(3):
            remote(slot, slot, out_s.at[2], ax_r.at[j], x_to[i]).start()

    def arrive_states(j):
        three = augx.at[0, 0:3]
        remote(three, three, out_s.at[2], ax_r.at[j], sib).wait_recv()

    send_weights(0)
    send_states(0)
    send_weights(1)
    for j in (1, 2, 3):
        send_states(j)
    arrive_weights(0)

    def share(target):
        states = augx[lax.rem(target, NG)].reshape(NX * 160, QT)
        weights = wx[lax.div(target, NG)].reshape(NX * 160, 2 * QT)
        return lax.dot_general(
            states, weights, (((0,), (0,)), ((), ())), preferred_element_type=jnp.float32
        )

    def send_p(k, kind, r):
        at = (k - 1, kind, r)
        remote(op.at[at], ip.at[at], out_s.at[3 + k // 4], rp_r.at[at], z_next).start()

    def send_m(k, kind, r):
        at = (k - 1, kind, r)
        remote(om.at[at], im.at[at], out_s.at[5 + k // 4], rm_r.at[at], z_prev).start()

    def got_p(k, kind, r):
        at = (k - 1, kind, r)
        remote(ip.at[at], ip.at[at], out_s.at[3 + k // 4], rp_r.at[at], z_next).wait_recv()
        return ip[at]

    def got_m(k, kind, r):
        at = (k - 1, kind, r)
        remote(im.at[at], im.at[at], out_s.at[5 + k // 4], rm_r.at[at], z_prev).wait_recv()
        return im[at]

    def fill(buf, k, part, halves=(0, 1)):
        for kind in (0, 1):
            for r in halves:
                buf[k - 1, kind, r] = part[r * HALF : (r + 1) * HALF, kind * QT : (kind + 1) * QT]

    arrive_states(0)
    part = share(wrap(z + 4, NZ))
    fill(op, 4, part, (0,))
    fill(om, 4, part, (1,))
    for kind in (0, 1):
        send_p(4, kind, 0)
        send_m(4, kind, 1)
    arrive_weights(1)
    arrive_states(1)
    fill(op, 3, share(wrap(z + 3, NZ)))
    for kind in (0, 1):
        send_p(3, kind, 1)
    arrive_states(2)
    fill(om, 3, share(wrap(z - 3, NZ)))
    for kind in (0, 1):
        send_m(3, kind, 0)
    for kind in (0, 1):
        op[2, kind, 0] += got_p(4, kind, 0)
        send_p(3, kind, 0)
        om[2, kind, 1] += got_m(4, kind, 1)
        send_m(3, kind, 1)
    arrive_states(3)
    fill(op, 2, share(wrap(z + 2, NZ)))
    fill(om, 2, share(wrap(z - 2, NZ)))
    fill(op, 1, share(wrap(z + 1, NZ)))
    fill(om, 1, share(wrap(z - 1, NZ)))
    own[...] = share(z)
    for k in (3, 2):
        for kind in (0, 1):
            for first in (0, 1):
                rp, rm = 1 - first, first
                op[k - 2, kind, rp] += got_p(k, kind, rp)
                send_p(k - 1, kind, rp)
                om[k - 2, kind, rm] += got_m(k, kind, rm)
                send_m(k - 1, kind, rm)

    def finish(kind):
        for r in (0, 1):
            rows = slice(r * HALF, (r + 1) * HALF)
            total = own[rows, kind * QT : (kind + 1) * QT] + got_m(1, kind, r) + got_p(1, kind, r)
            kvs[y, g, c, kind, rows] = total.astype(jnp.bfloat16)

    def quarter_of_own(e, qt):
        slot = kvs.at[y, qt, c]
        return remote(slot, slot, out_s.at[7], zg_r.at[e - 1], g_to[e - 1])

    units = (g, g2, g3)
    far = wrap(y + 4, NY)

    def ring_p(d, u):
        slot = kvs.at[wrap(y - d, NY), units[u], c]
        return remote(slot, slot, out_s.at[8], yp_r.at[d, u], y_next)

    def ring_m(d, u):
        slot = kvs.at[wrap(y + d, NY), units[u], c]
        return remote(slot, slot, out_s.at[9], ym_r.at[d, u], y_prev)

    def arrive_p(d, u):
        slot = kvs.at[wrap(y - d, NY), units[u], c]
        remote(slot, slot, out_s.at[8], yp_r.at[d - 1, u], y_next).wait_recv()

    def arrive_m(d, u):
        slot = kvs.at[wrap(y + d, NY), units[u], c]
        remote(slot, slot, out_s.at[9], ym_r.at[d - 1, u], y_prev).wait_recv()

    def swap(yi, d):
        slot = kvs.at[yi, g, c]
        remote(slot, slot, out_s.at[10], zq_r.at[d - 1], g_to[0]).start()

    def far_own():
        slot = kvs.at[far, g, c]
        return remote(slot, slot, out_s.at[11], far_r.at[0], across)

    def far_quarter(e, qt):
        slot = kvs.at[far, qt, c]
        return remote(slot, slot, out_s.at[7], far_r.at[e], g_to[e - 1])

    def share_core(group, yi, qt):
        slot = kvs.at[yi, qt, c]
        remote(slot, slot, out_s.at[12], sb_r.at[group], sib).start()

    def from_sibling(group):
        four = kvs.at[0, :, 0]
        remote(four, four, out_s.at[12], sb_r.at[group], sib).wait_recv()

    def own_unit(u):
        quarter_of_own(u + 1, units[u]).wait_recv()
        ring_p(0, u).start()
        ring_m(0, u).start()
        share_core(0, y, units[u])

    for kind in (0, 1):
        finish(kind)
        slot = kvs.at[y, g, c, kind]
        remote(slot, slot, out_s.at[8], yp_r.at[0, 0], y_next).start()
        remote(slot, slot, out_s.at[9], ym_r.at[0, 0], y_prev).start()
        for e in (2, 3, 1):
            remote(slot, slot, out_s.at[7], zg_r.at[e - 1], g_to[e - 1]).start()
    mine = kvs.at[y, g, c]
    remote(mine, mine, out_s.at[11], far_r.at[0], across).start()
    share_core(0, y, g)
    loads[2].wait()

    scale = LOG2E * 128 ** -0.5
    scores = (sc0, sc1)

    def score(pairs, rb, s, diagonal):
        q = q_ref[rb * ROWS : (rb + 1) * ROWS, :]
        qo = order_ref[2 * seq + rb * ROWS // 512]
        if diagonal:
            row = lax.broadcasted_iota(jnp.int32, (ROWS, QT), 0) + (rb * ROWS) % 512
            ahead = lax.shift_right_logical(row, 1) - lax.broadcasted_iota(jnp.int32, (ROWS, QT), 1)
        for h, (yi, qt) in enumerate(pairs):
            keys = jnp.concatenate([kvs[yi, qt, 0, 0], kvs[yi, qt, 1, 0]], axis=0)
            both = lax.dot_general(q, keys, (((1,), (1,)), ((), ())), preferred_element_type=jnp.float32) * scale
            for ci in (0, 1):
                place = order_ref[4 * yi + 2 * ci + lax.div(qt, 2)]
                part = both[:, ci * QT : (ci + 1) * QT]
                if diagonal:
                    part = jnp.where(ahead >= (place - qo) * 256 + lax.rem(qt, 2) * QT, part, NEG)
                else:
                    part = part + jnp.where(place < qo, 0.0, NEG)
                s[:, (2 * h + ci) * QT : (2 * h + ci + 1) * QT] = part

    def weigh(pairs, rb, s, diagonal):
        rows = slice(rb * ROWS, (rb + 1) * ROWS)
        parts = [s[:, i * QT : (i + 1) * QT] for i in range(2 * len(pairs))]
        top = functools.reduce(jnp.maximum, parts)
        new = jnp.broadcast_to(jnp.max(top, axis=-1, keepdims=True), (ROWS, QT))
        if not diagonal:
            old = m_ref[rows, :]
            new = jnp.maximum(old, new)
        m_ref[rows, :] = new
        total, o = None, None
        for h, (yi, qt) in enumerate(pairs):
            pair = [jnp.exp2(parts[2 * h + ci] - new) for ci in (0, 1)]
            t = pair[0] + pair[1]
            total = t if total is None else total + t
            probs = jnp.concatenate([v.astype(jnp.bfloat16) for v in pair], axis=1)
            values = jnp.concatenate([kvs[yi, qt, 0, 1], kvs[yi, qt, 1, 1]], axis=0)
            t = jnp.dot(probs, values, preferred_element_type=jnp.float32)
            o = t if o is None else o + t
        if diagonal:
            l_ref[rows, :] = total
            acc_ref[rows, :] = o
        else:
            alpha = jnp.exp2(old - new)
            l_ref[rows, :] = l_ref[rows, :] * alpha + total
            acc_ref[rows, :] = acc_ref[rows, :] * alpha + o

    def pairs_of(d, first):
        behind, before = wrap(y - d, NY), wrap(y + d, NY)
        return [(yi, qt) for qt in ((g, g2) if first else (g3, g1)) for yi in (behind, before)]

    chunks = [[(y, qt) for qt in range(NG)]]
    for d in (1, 2, 3):
        chunks += [pairs_of(d, True), pairs_of(d, False)]
    chunks.insert(4, [(far, qt) for qt in (g, g1, g2, g3)])
    state = {"next": 0, "scored": 0, "ready": 0}

    def ready(group):
        from_sibling(group)
        state["ready"] += 4

    def work(count):
        for _ in range(count):
            k = state["next"]
            while state["scored"] < min(k + 2, state["ready"]):
                n = state["scored"]
                score(chunks[n // 4], n % 4, scores[n % 2], n < 4)
                state["scored"] += 1
            weigh(chunks[k // 4], k % 4, scores[k % 2], k < 4)
            state["next"] += 1

    def unit(d, u):
        new_p, new_m = wrap(y - d, NY), wrap(y + d, NY)
        group = 2 * d - (1 if u < 2 else 0)
        arrive_p(d, u)
        if d < 3:
            ring_p(d, u).start()
        if u == 0:
            swap(new_p, d)
        share_core(group, new_p, units[u])
        arrive_m(d, u)
        if d < 3:
            ring_m(d, u).start()
        if u == 0:
            swap(new_m, d)
        share_core(group, new_m, units[u])

    def swapped(d):
        two = kvs.at[y, 0:2, c]
        remote(two, two, out_s.at[10], zq_r.at[d - 1], sib).wait_recv()
        share_core(2 * d, wrap(y - d, NY), g1)
        share_core(2 * d, wrap(y + d, NY), g1)

    own_unit(1)
    unit(1, 0)
    own_unit(2)
    quarter_of_own(1, g1).wait_recv()
    share_core(0, y, g1)
    far_own().wait_recv()
    for e in (2, 3, 1):
        far_quarter(e, g).start()
    share_core(7, far, g)
    ready(0)
    work(2)
    unit(2, 0)
    unit(1, 1)
    work(1)
    swapped(1)
    unit(1, 2)
    work(1)
    ready(1)
    work(2)
    unit(3, 0)
    work(1)
    unit(2, 1)
    swapped(2)
    ready(2)
    work(2)
    unit(2, 2)
    work(3)
    ready(3)
    work(1)
    for e, qt in ((1, g1), (2, g2), (3, g3)):
        far_quarter(e, qt).wait_recv()
        share_core(7, far, qt)
    unit(3, 1)
    swapped(3)
    work(3)
    ready(7)
    work(2)
    unit(3, 2)
    work(2)
    for group in (4, 5, 6):
        ready(group)
        work(4)

    out_ref[...] = (acc_ref[...] / jnp.sum(l_ref[...], axis=-1, keepdims=True)).astype(jnp.bfloat16)

    sent = [
        w_heads.at[0:3],
        w_heads.at[0:3],
        augx.at[0:3],
        op.at[0:3],
        op.at[3, :, 0],
        om.at[0:3],
        om.at[3, :, 1],
        kvs.at[0:2, 0:3, 0],
        kvs.at[0:3, 0:3, 0],
        kvs.at[0:3, 0:3, 0],
        kvs.at[0:3, 0:2, 0],
        kvs.at[0, 0, 0],
        kvs.at[:, :, 0],
    ]
    for i, ref in enumerate(sent):
        remote(ref, ref, out_s.at[i], far_r.at[0], sib).wait_send()


def body(queries, aug_states, key_value_weight, block_order):
    tok = queries.shape[0]
    rows = tok * queries.shape[2]
    q = queries.reshape(rows, 128)
    aug = aug_states.T
    w = key_value_weight.reshape(2560, 128)
    dma = pltpu.SemaphoreType.DMA
    out = pl.pallas_call(
        kernel,
        out_shape=jax.ShapeDtypeStruct((rows, 128), jnp.bfloat16),
        in_specs=[pl.BlockSpec(memory_space=pltpu.SMEM)] + [pl.BlockSpec(memory_space=pltpu.HBM)] * 3,
        out_specs=pl.BlockSpec(memory_space=pltpu.VMEM),
        scratch_shapes=[
            pltpu.VMEM((rows, 128), jnp.bfloat16),
            pltpu.VMEM((160, 512), jnp.bfloat16),
            pltpu.VMEM((2560, 128), jnp.bfloat16),
            pltpu.VMEM((2560, 128), jnp.float32),
            pltpu.VMEM((8, 160, 2 * QT), jnp.bfloat16),
            pltpu.VMEM((NG, NX, 160, QT), jnp.bfloat16),
            pltpu.VMEM((2, NX, 160, 2 * QT), jnp.bfloat16),
            pltpu.VMEM((4, 2, 2, HALF, QT), jnp.float32),
            pltpu.VMEM((4, 2, 2, HALF, QT), jnp.float32),
            pltpu.VMEM((4, 2, 2, HALF, QT), jnp.float32),
            pltpu.VMEM((4, 2, 2, HALF, QT), jnp.float32),
            pltpu.VMEM((QT, 2 * QT), jnp.float32),
            pltpu.VMEM((NY, NG, 2, 2, QT, QT), jnp.bfloat16),
            pltpu.VMEM((rows, 128), jnp.float32),
            pltpu.VMEM((rows, 128), jnp.float32),
            pltpu.VMEM((rows, 128), jnp.float32),
            pltpu.VMEM((ROWS, 8 * QT), jnp.float32),
            pltpu.VMEM((ROWS, 8 * QT), jnp.float32),
            dma((13,)),
            dma((4,)),
            dma((2,)),
            dma((2,)),
            dma((4, 2, 2)),
            dma((4, 2, 2)),
            dma((3,)),
            dma((3,)),
            dma((3, 3)),
            dma((3, 3)),
            dma((4,)),
            dma((8,)),
            dma((3,)),
        ],
        compiler_params=pltpu.CompilerParams(
            collective_id=0, has_side_effects=True, vmem_limit_bytes=62 * 1024 * 1024
        ),
        cost_estimate=pl.CostEstimate(flops=9 * 10**9, bytes_accessed=2 * 10**6, transcendentals=8 * 10**6),
        name="compose",
    )(block_order, q, aug, w)
    return out.reshape(queries.shape)


def solution(mesh):
    in_specs = (
        P("seq", "tp", "group", None),
        P("seq", ("group", "tp")),
        P(("group", "tp"), None, None, None),
        P(),
    )
    out_specs = P("seq", "tp", "group", None)
    return jax.shard_map(body, mesh=mesh, in_specs=in_specs, out_specs=out_specs, check_vma=False)
```

```python
import functools

import jax
import jax.numpy as jnp
from jax import lax
from jax.experimental import pallas as pl
from jax.experimental.pallas import tpu as pltpu
from jax.sharding import PartitionSpec as P

MESH = pl.DeviceIdType.MESH
NX, NY, NZ, NG = 4, 8, 8, 4
QT = 128
HALF = 64
ROWS = 256
NEG = -1e30
LOG2E = 1.4426950408889634


def kernel(
    order_ref,
    q_hbm,
    aug_hbm,
    w_hbm,
    out_ref,
    q_ref,
    aug_ref,
    w_ref,
    w_wide,
    w_heads,
    augx,
    wx,
    op,
    om,
    ip,
    im,
    own,
    kvs,
    m_ref,
    l_ref,
    acc_ref,
    sc0,
    sc1,
    out_s,
    ax_r,
    wx_r,
    ws_r,
    rp_r,
    rm_r,
    zg_r,
    zq_r,
    yp_r,
    ym_r,
    far_r,
    sb_r,
    loc,
):
    g = lax.axis_index("group")
    seq = lax.axis_index("seq")
    tp = lax.axis_index("tp")
    y, c = lax.div(seq, 2), lax.rem(seq, 2)
    zh, x = lax.div(tp, NX), lax.rem(tp, NX)
    z = zh * NG + g

    def dev(z=z, y=y, c=c, x=x):
        return (lax.rem(z, NG), y * 2 + c, lax.div(z, NG) * NX + x)

    def remote(src, dst, send, recv, to):
        return pltpu.make_async_remote_copy(
            src_ref=src, dst_ref=dst, send_sem=send, recv_sem=recv, device_id=to, device_id_type=MESH
        )

    def wrap(v, n):
        return lax.rem(v + 4 * n, n)

    x_to = [dev(x=wrap(x + d, NX)) for d in (1, 2, 3)]
    z_next, z_prev = dev(z=wrap(z + 1, NZ)), dev(z=wrap(z - 1, NZ))
    g1, g2, g3 = g + 1 - 2 * lax.rem(g, 2), lax.rem(g + 2, NG), 3 - g
    g_to = [dev(z=zh * NG + v) for v in (g1, g2, g3)]
    y_next, y_prev = dev(y=wrap(y + 1, NY)), dev(y=wrap(y - 1, NY))
    sib = dev(c=1 - c)
    across = dev(y=wrap(y + 4, NY))

    barrier = pltpu.get_barrier_semaphore()
    partners = [z_next, z_prev] + g_to + [across, y_next, y_prev] + x_to + [sib]
    for to in partners:
        pl.semaphore_signal(barrier, inc=1, device_id=to, device_id_type=MESH)

    loads = [
        pltpu.make_async_copy(w_hbm, w_ref, loc.at[0]),
        pltpu.make_async_copy(aug_hbm, aug_ref, loc.at[1]),
        pltpu.make_async_copy(q_hbm, q_ref, loc.at[2]),
    ]
    for cp in loads:
        cp.start()
    loads[0].wait()
    w_wide[0:2560, :] = w_ref[...].astype(jnp.float32)
    for j in range(8):
        for half in (0, 1):
            w_heads[j, :, half * QT : (half + 1) * QT] = w_wide[pl.ds(2 * j + half, 160, stride=16), :].astype(
                jnp.bfloat16
            )
    for h in (0, 1):
        wx[h, x] = w_heads[x + NX * h]
    loads[1].wait()
    for i in range(NG):
        augx[i, x] = aug_ref[:, i * QT : (i + 1) * QT]
    pl.semaphore_wait(barrier, len(partners))

    heads = (1 - zh, zh)
    band = pl.ds(pl.multiple_of(80 * c, 16), 80)

    def send_weights(n):
        for i, d in enumerate((1, 2, 3)):
            src = w_heads.at[wrap(x + d, NX) + NX * heads[n], band]
            remote(src, wx.at[heads[n], x, band], out_s.at[0], wx_r.at[n], x_to[i]).start()

    def arrive_weights(n):
        three = wx.at[0, 0:3, band]
        remote(three, three, out_s.at[0], wx_r.at[n], sib).wait_recv()
        for d in (1, 2, 3):
            slot = wx.at[heads[n], wrap(x - d, NX), band]
            remote(slot, slot, out_s.at[1], ws_r.at[n], sib).start()
        remote(three, three, out_s.at[1], ws_r.at[n], sib).wait_recv()

    quarters = [g, wrap(g - 1, NG), wrap(g + 1, NG), wrap(g + 2, NG)]

    def send_states(j):
        slot = augx.at[quarters[j], x]
        for i in range(3):
            remote(slot, slot, out_s.at[2], ax_r.at[j], x_to[i]).start()

    def arrive_states(j):
        three = augx.at[0, 0:3]
        remote(three, three, out_s.at[2], ax_r.at[j], sib).wait_recv()

    send_weights(0)
    send_states(0)
    send_weights(1)
    for j in (1, 2, 3):
        send_states(j)
    arrive_weights(0)

    def share(target):
        states = augx[lax.rem(target, NG)].reshape(NX * 160, QT)
        weights = wx[lax.div(target, NG)].reshape(NX * 160, 2 * QT)
        return lax.dot_general(
            states, weights, (((0,), (0,)), ((), ())), preferred_element_type=jnp.float32
        )

    def send_p(k, kind, r):
        at = (k - 1, kind, r)
        remote(op.at[at], ip.at[at], out_s.at[3 + k // 4], rp_r.at[at], z_next).start()

    def send_m(k, kind, r):
        at = (k - 1, kind, r)
        remote(om.at[at], im.at[at], out_s.at[5 + k // 4], rm_r.at[at], z_prev).start()

    def got_p(k, kind, r):
        at = (k - 1, kind, r)
        remote(ip.at[at], ip.at[at], out_s.at[3 + k // 4], rp_r.at[at], z_next).wait_recv()
        return ip[at]

    def got_m(k, kind, r):
        at = (k - 1, kind, r)
        remote(im.at[at], im.at[at], out_s.at[5 + k // 4], rm_r.at[at], z_prev).wait_recv()
        return im[at]

    def fill(buf, k, part, halves=(0, 1)):
        for kind in (0, 1):
            for r in halves:
                buf[k - 1, kind, r] = part[r * HALF : (r + 1) * HALF, kind * QT : (kind + 1) * QT]

    arrive_states(0)
    part = share(wrap(z + 4, NZ))
    fill(op, 4, part, (0,))
    fill(om, 4, part, (1,))
    for kind in (0, 1):
        send_p(4, kind, 0)
        send_m(4, kind, 1)
    arrive_weights(1)
    arrive_states(1)
    fill(op, 3, share(wrap(z + 3, NZ)))
    for kind in (0, 1):
        send_p(3, kind, 1)
    arrive_states(2)
    fill(om, 3, share(wrap(z - 3, NZ)))
    for kind in (0, 1):
        send_m(3, kind, 0)
    for kind in (0, 1):
        op[2, kind, 0] += got_p(4, kind, 0)
        send_p(3, kind, 0)
        om[2, kind, 1] += got_m(4, kind, 1)
        send_m(3, kind, 1)
    arrive_states(3)
    fill(op, 2, share(wrap(z + 2, NZ)))
    fill(om, 2, share(wrap(z - 2, NZ)))
    fill(op, 1, share(wrap(z + 1, NZ)))
    fill(om, 1, share(wrap(z - 1, NZ)))
    own[...] = share(z)
    for k in (3, 2):
        for kind in (0, 1):
            for first in (0, 1):
                rp, rm = 1 - first, first
                op[k - 2, kind, rp] += got_p(k, kind, rp)
                send_p(k - 1, kind, rp)
                om[k - 2, kind, rm] += got_m(k, kind, rm)
                send_m(k - 1, kind, rm)

    def finish(kind):
        for r in (0, 1):
            rows = slice(r * HALF, (r + 1) * HALF)
            total = own[rows, kind * QT : (kind + 1) * QT] + got_m(1, kind, r) + got_p(1, kind, r)
            kvs[y, g, c, kind, rows] = total.astype(jnp.bfloat16)

    def quarter_of_own(e, qt):
        slot = kvs.at[y, qt, c]
        return remote(slot, slot, out_s.at[7], zg_r.at[e - 1], g_to[e - 1])

    units = (g, g2, g3)
    far = wrap(y + 4, NY)

    def ring_p(d, u):
        slot = kvs.at[wrap(y - d, NY), units[u], c]
        return remote(slot, slot, out_s.at[8], yp_r.at[d, u], y_next)

    def ring_m(d, u):
        slot = kvs.at[wrap(y + d, NY), units[u], c]
        return remote(slot, slot, out_s.at[9], ym_r.at[d, u], y_prev)

    def arrive_p(d, u):
        slot = kvs.at[wrap(y - d, NY), units[u], c]
        remote(slot, slot, out_s.at[8], yp_r.at[d - 1, u], y_next).wait_recv()

    def arrive_m(d, u):
        slot = kvs.at[wrap(y + d, NY), units[u], c]
        remote(slot, slot, out_s.at[9], ym_r.at[d - 1, u], y_prev).wait_recv()

    def swap(yi, d):
        slot = kvs.at[yi, g, c]
        remote(slot, slot, out_s.at[10], zq_r.at[d - 1], g_to[0]).start()

    def far_own():
        slot = kvs.at[far, g, c]
        return remote(slot, slot, out_s.at[11], far_r.at[0], across)

    def far_quarter(e, qt):
        slot = kvs.at[far, qt, c]
        return remote(slot, slot, out_s.at[7], far_r.at[e], g_to[e - 1])

    def share_core(group, yi, qt):
        slot = kvs.at[yi, qt, c]
        remote(slot, slot, out_s.at[12], sb_r.at[group], sib).start()

    def from_sibling(group):
        four = kvs.at[0, :, 0]
        remote(four, four, out_s.at[12], sb_r.at[group], sib).wait_recv()

    def own_unit(u):
        quarter_of_own(u + 1, units[u]).wait_recv()
        ring_p(0, u).start()
        ring_m(0, u).start()
        share_core(0, y, units[u])

    for kind in (0, 1):
        finish(kind)
        slot = kvs.at[y, g, c, kind]
        remote(slot, slot, out_s.at[8], yp_r.at[0, 0], y_next).start()
        remote(slot, slot, out_s.at[9], ym_r.at[0, 0], y_prev).start()
        for e in (2, 3, 1):
            remote(slot, slot, out_s.at[7], zg_r.at[e - 1], g_to[e - 1]).start()
    mine = kvs.at[y, g, c]
    remote(mine, mine, out_s.at[11], far_r.at[0], across).start()
    share_core(0, y, g)
    loads[2].wait()

    scale = LOG2E * 128 ** -0.5
    scores = (sc0, sc1)

    def score(pairs, rb, s, diagonal):
        q = q_ref[rb * ROWS : (rb + 1) * ROWS, :]
        qo = order_ref[2 * seq + rb * ROWS // 512]
        if diagonal:
            row = lax.broadcasted_iota(jnp.int32, (ROWS, QT), 0) + (rb * ROWS) % 512
            ahead = lax.shift_right_logical(row, 1) - lax.broadcasted_iota(jnp.int32, (ROWS, QT), 1)
        for h, (yi, qt) in enumerate(pairs):
            keys = jnp.concatenate([kvs[yi, qt, 0, 0], kvs[yi, qt, 1, 0]], axis=0)
            both = lax.dot_general(q, keys, (((1,), (1,)), ((), ())), preferred_element_type=jnp.float32) * scale
            for ci in (0, 1):
                place = order_ref[4 * yi + 2 * ci + lax.div(qt, 2)]
                part = both[:, ci * QT : (ci + 1) * QT]
                if diagonal:
                    part = jnp.where(ahead >= (place - qo) * 256 + lax.rem(qt, 2) * QT, part, NEG)
                else:
                    part = part + jnp.where(place < qo, 0.0, NEG)
                s[:, (2 * h + ci) * QT : (2 * h + ci + 1) * QT] = part

    def weigh(pairs, rb, s, diagonal):
        rows = slice(rb * ROWS, (rb + 1) * ROWS)
        parts = [s[:, i * QT : (i + 1) * QT] for i in range(2 * len(pairs))]
        top = functools.reduce(jnp.maximum, parts)
        new = jnp.broadcast_to(jnp.max(top, axis=-1, keepdims=True), (ROWS, QT))
        if not diagonal:
            old = m_ref[rows, :]
            new = jnp.maximum(old, new)
        m_ref[rows, :] = new
        total, o = None, None
        for h, (yi, qt) in enumerate(pairs):
            pair = [jnp.exp2(parts[2 * h + ci] - new) for ci in (0, 1)]
            t = pair[0] + pair[1]
            total = t if total is None else total + t
            probs = jnp.concatenate([v.astype(jnp.bfloat16) for v in pair], axis=1)
            values = jnp.concatenate([kvs[yi, qt, 0, 1], kvs[yi, qt, 1, 1]], axis=0)
            t = jnp.dot(probs, values, preferred_element_type=jnp.float32)
            o = t if o is None else o + t
        if diagonal:
            l_ref[rows, :] = total
            acc_ref[rows, :] = o
        else:
            alpha = jnp.exp2(old - new)
            l_ref[rows, :] = l_ref[rows, :] * alpha + total
            acc_ref[rows, :] = acc_ref[rows, :] * alpha + o

    def pairs_of(d, first):
        behind, before = wrap(y - d, NY), wrap(y + d, NY)
        return [(yi, qt) for qt in ((g, g2) if first else (g3, g1)) for yi in (behind, before)]

    chunks = [[(y, qt) for qt in range(NG)]]
    for d in (1, 2, 3):
        chunks += [pairs_of(d, True), pairs_of(d, False)]
    chunks.insert(4, [(far, qt) for qt in (g, g1, g2, g3)])
    state = {"next": 0, "scored": 0, "ready": 0}

    def ready(group):
        from_sibling(group)
        state["ready"] += 4

    def work(count):
        for _ in range(count):
            k = state["next"]
            while state["scored"] < min(k + 2, state["ready"]):
                n = state["scored"]
                score(chunks[n // 4], n % 4, scores[n % 2], n < 4)
                state["scored"] += 1
            weigh(chunks[k // 4], k % 4, scores[k % 2], k < 4)
            state["next"] += 1

    def unit(d, u):
        new_p, new_m = wrap(y - d, NY), wrap(y + d, NY)
        group = 2 * d - (1 if u < 2 else 0)
        arrive_p(d, u)
        if d < 3:
            ring_p(d, u).start()
        if u == 0:
            swap(new_p, d)
        share_core(group, new_p, units[u])
        arrive_m(d, u)
        if d < 3:
            ring_m(d, u).start()
        if u == 0:
            swap(new_m, d)
        share_core(group, new_m, units[u])

    def swapped(d):
        two = kvs.at[y, 0:2, c]
        remote(two, two, out_s.at[10], zq_r.at[d - 1], sib).wait_recv()
        share_core(2 * d, wrap(y - d, NY), g1)
        share_core(2 * d, wrap(y + d, NY), g1)

    own_unit(1)
    unit(1, 0)
    own_unit(2)
    quarter_of_own(1, g1).wait_recv()
    share_core(0, y, g1)
    far_own().wait_recv()
    for e in (2, 3, 1):
        far_quarter(e, g).start()
    share_core(7, far, g)
    ready(0)
    work(2)
    unit(2, 0)
    unit(1, 1)
    work(1)
    swapped(1)
    unit(1, 2)
    work(1)
    ready(1)
    work(2)
    unit(3, 0)
    work(1)
    unit(2, 1)
    swapped(2)
    ready(2)
    work(2)
    unit(2, 2)
    work(3)
    ready(3)
    work(1)
    for e, qt in ((1, g1), (2, g2), (3, g3)):
        far_quarter(e, qt).wait_recv()
        share_core(7, far, qt)
    unit(3, 1)
    swapped(3)
    work(3)
    ready(7)
    work(2)
    unit(3, 2)
    work(2)
    for group in (4, 5, 6):
        ready(group)
        work(4)

    out_ref[...] = (acc_ref[...] / jnp.sum(l_ref[...], axis=-1, keepdims=True)).astype(jnp.bfloat16)

    sent = [
        w_heads.at[0:3],
        w_heads.at[0:3],
        augx.at[0:3],
        op.at[0:3],
        op.at[3, :, 0],
        om.at[0:3],
        om.at[3, :, 1],
        kvs.at[0:2, 0:3, 0],
        kvs.at[0:3, 0:3, 0],
        kvs.at[0:3, 0:3, 0],
        kvs.at[0:3, 0:2, 0],
        kvs.at[0, 0, 0],
        kvs.at[:, :, 0],
    ]
    for i, ref in enumerate(sent):
        remote(ref, ref, out_s.at[i], far_r.at[0], sib).wait_send()


def body(queries, aug_states, key_value_weight, block_order):
    tok = queries.shape[0]
    rows = tok * queries.shape[2]
    q = queries.reshape(rows, 128)
    aug = aug_states.T
    w = key_value_weight.reshape(2560, 128)
    dma = pltpu.SemaphoreType.DMA
    out = pl.pallas_call(
        kernel,
        out_shape=jax.ShapeDtypeStruct((rows, 128), jnp.bfloat16),
        in_specs=[pl.BlockSpec(memory_space=pltpu.SMEM)] + [pl.BlockSpec(memory_space=pltpu.HBM)] * 3,
        out_specs=pl.BlockSpec(memory_space=pltpu.VMEM),
        scratch_shapes=[
            pltpu.VMEM((rows, 128), jnp.bfloat16),
            pltpu.VMEM((160, 512), jnp.bfloat16),
            pltpu.VMEM((2560, 128), jnp.bfloat16),
            pltpu.VMEM((2576, 128), jnp.float32),
            pltpu.VMEM((8, 160, 2 * QT), jnp.bfloat16),
            pltpu.VMEM((NG, NX, 160, QT), jnp.bfloat16),
            pltpu.VMEM((2, NX, 160, 2 * QT), jnp.bfloat16),
            pltpu.VMEM((4, 2, 2, HALF, QT), jnp.float32),
            pltpu.VMEM((4, 2, 2, HALF, QT), jnp.float32),
            pltpu.VMEM((4, 2, 2, HALF, QT), jnp.float32),
            pltpu.VMEM((4, 2, 2, HALF, QT), jnp.float32),
            pltpu.VMEM((QT, 2 * QT), jnp.float32),
            pltpu.VMEM((NY, NG, 2, 2, QT, QT), jnp.bfloat16),
            pltpu.VMEM((rows, 128), jnp.float32),
            pltpu.VMEM((rows, 128), jnp.float32),
            pltpu.VMEM((rows, 128), jnp.float32),
            pltpu.VMEM((ROWS, 8 * QT), jnp.float32),
            pltpu.VMEM((ROWS, 8 * QT), jnp.float32),
            dma((13,)),
            dma((4,)),
            dma((2,)),
            dma((2,)),
            dma((4, 2, 2)),
            dma((4, 2, 2)),
            dma((3,)),
            dma((3,)),
            dma((3, 3)),
            dma((3, 3)),
            dma((4,)),
            dma((8,)),
            dma((3,)),
        ],
        compiler_params=pltpu.CompilerParams(
            collective_id=0, has_side_effects=True, vmem_limit_bytes=62 * 1024 * 1024
        ),
        cost_estimate=pl.CostEstimate(flops=9 * 10**9, bytes_accessed=2 * 10**6, transcendentals=8 * 10**6),
        name="compose",
    )(block_order, q, aug, w)
    return out.reshape(queries.shape)


def solution(mesh):
    in_specs = (
        P("seq", "tp", "group", None),
        P("seq", ("group", "tp")),
        P(("group", "tp"), None, None, None),
        P(),
    )
    out_specs = P("seq", "tp", "group", None)
    return jax.shard_map(body, mesh=mesh, in_specs=in_specs, out_specs=out_specs, check_vma=False)
```
